256 devices in a mesh: wide: 128 (over z, y, x), narrow: 2 (over core).
Axes of the slice: x: 4, y: 4, z: 8, core: 2. Of those that a mesh axis runs over, the one named last changes fastest.
Arguments:
- rhs: float32 [3072, 64, 128], P(('wide', 'narrow')), may hold values from -8 to 8
- pivot_inv: float32 [3072, 128, 128], P(('wide', 'narrow')), may hold values from -0.5 to 0.5
- lower_gain: float32 [3072, 128, 128], P(('wide', 'narrow')), may hold values from -1 to 1
- upper_gain: float32 [3072, 128, 128], P(('wide', 'narrow')), may hold values from -1 to 1
Outputs:
- solution: float32 [3072, 64, 128], P(('wide', 'narrow'))
The draws below stay inside these ranges and needn't reach their ends.
All inputs are finite; a program needn't handle non-finite values.
Results may differ from the reference program's by a relative error of at most 0.0003.
Values sent between devices are 32-bit elements; how exact they have to be, the bound alone decides.
No kernel may reach another device: no remote copies, remote signals or barrier semaphores. Data moves between devices by JAX's collectives and lax.ppermute only.
A program may use at most 128 MiB of HBM per device.

```python
import math
import jax
import jax.numpy as jnp
from jax import lax

B = 128
R = 64
PANEL_COUNT_FULL = 3072


def rotation_frames(key, count):
    levels = B.bit_length() - 1
    angles = jax.random.uniform(key, (2 * levels, count, B // 2), minval=-math.pi, maxval=math.pi)
    basis = jnp.broadcast_to(jnp.eye(B, dtype=jnp.float32), (count, B, B))
    for segment in range(2 * levels):
        stride = 2 ** (segment % levels)
        shaped = basis.reshape(count, B, B // (2 * stride), 2, stride)
        turn = angles[segment].reshape(count, 1, B // (2 * stride), stride)
        cosine = jnp.cos(turn)
        sine = jnp.sin(turn)
        first = shaped[:, :, :, 0, :]
        second = shaped[:, :, :, 1, :]
        basis = jnp.stack((cosine * first - sine * second, sine * first + cosine * second), axis=3).reshape(count, B, B)
    return basis


def gain_stack(key, slow_eighths, spread, ascending):
    sampler_seeds = jax.random.split(key, 7)
    gradual_portion = (jax.random.randint(sampler_seeds[0], (B,), 0, 8) < slow_eighths).astype(jnp.float32)
    slow_rate = 1.0 / (PANEL_COUNT_FULL * jnp.exp(jax.random.uniform(sampler_seeds[1], (B,), minval=0.0, maxval=math.log(6.0))))
    fast_rate = jnp.exp(jax.random.uniform(sampler_seeds[2], (B,), minval=math.log(0.02), maxval=math.log(0.2)))
    attenuation_speed = gradual_portion * slow_rate + (1.0 - gradual_portion) * fast_rate
    perturbation_magnitude = jax.random.uniform(sampler_seeds[3], (PANEL_COUNT_FULL, B), minval=1.0 - spread, maxval=1.0 + spread)
    spike_multiplier = jnp.where(jax.random.uniform(sampler_seeds[4], (PANEL_COUNT_FULL, 1)) < 3.0 / PANEL_COUNT_FULL, 0.7, 1.0)
    shrinkage_multiplier = jnp.exp(-attenuation_speed * perturbation_magnitude) * (gradual_portion * spike_multiplier + 1.0 - gradual_portion)
    frames = rotation_frames(sampler_seeds[5], PANEL_COUNT_FULL + 1)
    if ascending:
        left_frame = frames[:-1]
        right_frame = frames[1:]
    else:
        left_frame = frames[1:]
        right_frame = frames[:-1]
    core = jnp.einsum('kij,klj->kil', left_frame * shrinkage_multiplier[:, None, :], right_frame, precision=lax.Precision.HIGHEST)
    jitter = jax.random.normal(sampler_seeds[6], (PANEL_COUNT_FULL, B, B)) * (0.5 / math.sqrt(PANEL_COUNT_FULL * B))
    return jnp.clip(core + jitter, -1.0, 1.0).astype(jnp.float32)


def draw_lower_gain(key, part):
    key = jax.random.fold_in(key, 3)
    return gain_stack(key, 4, 0.5, True)


def draw_upper_gain(key, part):
    key = jax.random.fold_in(key, 5)
    return gain_stack(key, 4, 0.5, False)


def block_scale(key, extent, cuts, least, largest):
    def one(position, shards_of):
        heights = jax.random.uniform(jax.random.fold_in(jax.random.fold_in(key, 6), position), (shards_of,), jnp.float32, least / len(cuts), largest / len(cuts))
        return jnp.repeat(jnp.exp(heights), extent[position] // shards_of).reshape((-1,) + (1,) * (len(extent) - position - 1))

    level = one(*cuts[0])
    for cut in cuts[1:]:
        level = level * one(*cut)
    return level


def centred(rng, shape, deviation, reach, cuts=(), kind=jnp.bfloat16):
    values = deviation * jax.random.normal(rng, shape, jnp.float32)
    if cuts:
        values = values * block_scale(rng, shape, cuts, -0.22, 0.18)
    return jnp.clip(values, -reach, reach).astype(kind)


def setup_inputs(seed: int = 0) -> dict:
    key_list = jax.random.split(jax.random.key(seed), 5)
    return {
        "rhs": centred(key_list[0], (PANEL_COUNT_FULL, R, B), 1.0, 8.0, ((0, 256),), jnp.float32),
        "pivot_inv": centred(key_list[1], (PANEL_COUNT_FULL, B, B), B ** -0.5, 0.5, ((0, 256),), jnp.float32),
        "lower_gain": draw_lower_gain(jax.random.fold_in(key_list[4], 71), 0),
        "upper_gain": draw_upper_gain(jax.random.fold_in(key_list[4], 71), 0),
    }


def reference(rhs, pivot_inv, lower_gain, upper_gain):
    highest = lax.Precision.HIGHEST
    scaled = jnp.einsum("krb,kbc->krc", rhs, pivot_inv, precision=highest)

    def stepper(carry, item):
        gain, offset = item
        fresh = offset - jnp.dot(carry, gain, precision=highest)
        return fresh, fresh

    start = jnp.zeros((rhs.shape[1], rhs.shape[2]), jnp.float32)
    _, forward = lax.scan(stepper, start, (lower_gain, scaled))
    _, solution = lax.scan(stepper, start, (upper_gain, forward), reverse=True)
    return solution
```

```python
import jax
import jax.numpy as jnp
from jax import lax
from jax.experimental import pallas as pl
from jax.experimental.pallas import tpu as pltpu
from jax.sharding import PartitionSpec as P

AXES = ("wide", "narrow")
B = 128
R = 64
PACK = 3 * B + 2 * R


def halves(value):
    high = value.astype(jnp.bfloat16)
    low = (value - high.astype(jnp.float32)).astype(jnp.bfloat16)
    return high, low


def left_side(value):
    return jnp.concatenate(halves(value), axis=1)


def right_side(value):
    both = jnp.concatenate(halves(value), axis=1)
    return jnp.concatenate([both, both], axis=0)


def times(left, right):
    wide = jnp.dot(left, right, preferred_element_type=jnp.float32)
    return wide[:, :B] + wide[:, B:]


def mm(left, right):
    return times(left_side(left), right_side(right))


def local_kernel(rhs, pivot_inv, lower, upper, pack, rows, forward):
    count = rhs.shape[0]
    scaled = [mm(rhs[i], pivot_inv[i]) for i in range(count)]
    state = jnp.concatenate([-lower[0], scaled[0]], axis=0)
    forward[0] = state
    for i in range(1, count):
        moved = mm(state, lower[i])
        state = jnp.concatenate([-moved[:B], scaled[i] - moved[B:]], axis=0)
        forward[i] = state
    pack[: B + R] = state
    state = jnp.concatenate([-upper[count - 1], state], axis=0)
    rows[count - 1] = state
    for i in range(count - 2, -1, -1):
        moved = mm(state, upper[i])
        state = jnp.concatenate([-moved[:B], forward[i] - moved[B:]], axis=0)
        rows[i] = state
    pack[B + R :] = state


def local(rhs, pivot_inv, lower, upper):
    count = rhs.shape[0]
    return pl.pallas_call(
        local_kernel,
        out_shape=(
            jax.ShapeDtypeStruct((PACK, B), jnp.float32),
            jax.ShapeDtypeStruct((count, 2 * B + R, B), jnp.float32),
        ),
        in_specs=[pl.BlockSpec(memory_space=pltpu.VMEM)] * 4,
        out_specs=[pl.BlockSpec(memory_space=pltpu.VMEM)] * 2,
        scratch_shapes=[pltpu.VMEM((count, B + R, B), jnp.float32)],
        compiler_params=pltpu.CompilerParams(vmem_limit_bytes=40 * 2**20),
        name="local",
    )(rhs, pivot_inv, lower, upper)


def position():
    return lax.axis_index(AXES[0]) * lax.axis_size(AXES[1]) + lax.axis_index(AXES[1])


def join_kernel(level, own, other, pack):
    left = (position() >> level) & 1 == 0

    def join(first, second):
        early = left_side(first[: B + R])
        down = times(early, right_side(second[:B]))
        pack[:B] = down[:B]
        pack[B : B + R] = down[B:] + second[B : B + R]
        turn = times(early, right_side(second[2 * B + R : 3 * B + R]))
        back = jnp.concatenate(
            [second[B + R : 2 * B + R], turn[:B], turn[B:] + second[3 * B + R :]], axis=0
        )
        up = mm(back, first[B + R : 2 * B + R])
        pack[B + R : 2 * B + R] = up[:B]
        pack[2 * B + R :] = up[B:] + first[2 * B + R :]

    @pl.when(left)
    def _():
        join(own, other)

    @pl.when(jnp.logical_not(left))
    def _():
        join(other, own)


def join(level, own, other):
    return pl.pallas_call(
        lambda *refs: join_kernel(level, *refs),
        out_shape=jax.ShapeDtypeStruct((PACK, B), jnp.float32),
        in_specs=[pl.BlockSpec(memory_space=pltpu.VMEM)] * 2,
        out_specs=pl.BlockSpec(memory_space=pltpu.VMEM),
        name=f"join{level}",
    )(own, other)


def finish_kernel(levels, *refs):
    rows, out = refs[2 * levels], refs[2 * levels + 1]
    ahead = jnp.zeros((R, B), jnp.float32)
    behind = jnp.zeros((R, B), jnp.float32)
    for level in range(levels - 1, -1, -1):
        own, other = refs[level], refs[levels + level]
        left = (position() >> level) & 1 == 0
        pick = lambda low, high: jnp.where(left, own[low:high], other[low:high])
        skip = lambda low, high: jnp.where(left, other[low:high], own[low:high])
        middle = mm(behind, pick(0, B)) + pick(B, B + R)
        moved = (
            mm(ahead, skip(B + R, 2 * B + R))
            + mm(middle, skip(2 * B + R, 3 * B + R))
            + skip(3 * B + R, PACK)
        )
        ahead = jnp.where(left, moved, ahead)
        behind = jnp.where(left, behind, middle)
    ahead, behind = left_side(ahead), left_side(behind)
    for i in range(out.shape[0]):
        out[i] = (
            rows[i, 2 * B :]
            + times(ahead, right_side(rows[i, :B]))
            + times(behind, right_side(rows[i, B : 2 * B]))
        )


def finish(owns, others, rows):
    levels = len(owns)
    return pl.pallas_call(
        lambda *refs: finish_kernel(levels, *refs),
        out_shape=jax.ShapeDtypeStruct((rows.shape[0], R, B), jnp.float32),
        in_specs=[pl.BlockSpec(memory_space=pltpu.VMEM)] * (2 * levels + 1),
        out_specs=pl.BlockSpec(memory_space=pltpu.VMEM),
        compiler_params=pltpu.CompilerParams(vmem_limit_bytes=40 * 2**20),
        name="finish",
    )(*owns, *others, rows)


def on_device(rhs, pivot_inv, lower_gain, upper_gain):
    devices = lax.axis_size(AXES)
    levels = devices.bit_length() - 1
    pack, rows = local(rhs, pivot_inv, lower_gain, upper_gain)
    owns, others = [], []
    for level in range(levels):
        other = lax.ppermute(pack, AXES, [(i, i ^ (1 << level)) for i in range(devices)])
        owns.append(pack)
        others.append(other)
        if level < levels - 1:
            pack = join(level, pack, other)
    return finish(owns, others, rows)


def solution(mesh):
    placed = P(AXES, None, None)
    return jax.shard_map(
        on_device,
        mesh=mesh,
        in_specs=(placed,) * 4,
        out_specs=placed,
        check_vma=False,
    )
```

```python
import jax
import jax.numpy as jnp
from jax import lax
from jax.experimental import pallas as pl
from jax.experimental.pallas import tpu as pltpu
from jax.sharding import PartitionSpec as P

AXES = ("wide", "narrow")
B = 128
R = 64
PACK = 3 * B + 2 * R
CHUNKS = 3
LIMIT = 12 * 2**20


def halves(value):
    high = value.astype(jnp.bfloat16)
    low = (value - high.astype(jnp.float32)).astype(jnp.bfloat16)
    return high, low


def left_side(value):
    return jnp.concatenate(halves(value), axis=1)


def right_side(value):
    both = jnp.concatenate(halves(value), axis=1)
    return jnp.concatenate([both, both], axis=0)


def times(left, right):
    wide = jnp.dot(left, right, preferred_element_type=jnp.float32)
    return wide[:, :B] + wide[:, B:]


def mm(left, right):
    return times(left_side(left), right_side(right))


def local_kernel(
    rhs_hbm, pivot_hbm, lower_hbm, upper_hbm, pack, rows, rhs, pivot_inv, lower, upper, forward, sems
):
    count = rhs.shape[0]
    pairs = ((pivot_hbm, pivot_inv), (rhs_hbm, rhs), (lower_hbm, lower), (upper_hbm, upper))
    chunk = count // CHUNKS
    copies = {}
    for part in range(CHUNKS):
        for which, (source, target) in enumerate(pairs):
            at = CHUNKS - 1 - part if which == 3 else part
            span = pl.ds(at * chunk, chunk)
            copy = pltpu.make_async_copy(source.at[span], target.at[span], sems.at[which, at])
            copy.start()
            copies[which, at] = copy
    scaled = []
    state = None
    for i in range(count):
        if i % chunk == 0:
            for which in range(3):
                copies[which, i // chunk].wait()
            scaled += [mm(rhs[j], pivot_inv[j]) for j in range(i, i + chunk)]
        if i == 0:
            state = jnp.concatenate([-lower[0], scaled[0]], axis=0)
        else:
            moved = mm(state, lower[i])
            state = jnp.concatenate([-moved[:B], scaled[i] - moved[B:]], axis=0)
        forward[i] = state
    pack[: B + R] = state
    for i in range(count - 1, -1, -1):
        if (i + 1) % chunk == 0:
            copies[3, i // chunk].wait()
        if i == count - 1:
            state = jnp.concatenate([-upper[i], state], axis=0)
        else:
            moved = mm(state, upper[i])
            state = jnp.concatenate([-moved[:B], forward[i] - moved[B:]], axis=0)
        rows[i] = state
    pack[B + R :] = state


def local(rhs, pivot_inv, lower, upper):
    count = rhs.shape[0]
    return pl.pallas_call(
        local_kernel,
        out_shape=(
            jax.ShapeDtypeStruct((PACK, B), jnp.float32),
            jax.ShapeDtypeStruct((count, 2 * B + R, B), jnp.float32),
        ),
        in_specs=[pl.BlockSpec(memory_space=pltpu.HBM)] * 4,
        out_specs=[pl.BlockSpec(memory_space=pltpu.VMEM)] * 2,
        scratch_shapes=[
            pltpu.VMEM(rhs.shape, jnp.float32),
            pltpu.VMEM(pivot_inv.shape, jnp.float32),
            pltpu.VMEM(lower.shape, jnp.float32),
            pltpu.VMEM(upper.shape, jnp.float32),
            pltpu.VMEM((count, B + R, B), jnp.float32),
            pltpu.SemaphoreType.DMA((4, CHUNKS)),
        ],
        compiler_params=pltpu.CompilerParams(vmem_limit_bytes=LIMIT),
        name="local",
    )(rhs, pivot_inv, lower, upper)


def position():
    return lax.axis_index(AXES[0]) * lax.axis_size(AXES[1]) + lax.axis_index(AXES[1])


def is_left(level):
    return (position() >> level) & 1 == 0


def ordered(level, own, other):
    left = is_left(level)
    return jnp.where(left, own, other), jnp.where(left, other, own)


def partner_pack(refs):
    if len(refs) == 1:
        return refs[0][...]
    here, there = refs[0][...], refs[1][...]
    low = position() & 1 == 0
    return jnp.concatenate([jnp.where(low, here, there), jnp.where(low, there, here)], axis=0)


def turned(first, second):
    early = left_side(first[: B + R])
    turn = times(early, right_side(second[2 * B + R : 3 * B + R]))
    back = jnp.concatenate(
        [second[B + R : 2 * B + R], turn[:B], turn[B:] + second[3 * B + R :]], axis=0
    )
    return early, back


def join_kernel(level, top, *refs):
    own, parts, (pack, send) = refs[0][...], refs[1:-2], refs[-2:]
    first, second = ordered(level, own, partner_pack(parts))
    early, back = turned(first, second)
    down = times(early, right_side(second[:B]))
    up = mm(back, first[B + R : 2 * B + R])
    ahead = jnp.concatenate([down[:B], down[B:] + second[B : B + R]], axis=0)
    behind = jnp.concatenate([up[:B], up[B:] + first[2 * B + R :]], axis=0)
    pack[: B + R] = ahead
    pack[B + R :] = behind
    if top:
        send[...] = jnp.where(is_left(level + 1), ahead, behind[B:])
    else:
        low = position() & 1 == 0
        half = PACK // 2
        send[: B + R] = jnp.where(low, ahead, behind[half - B - R : half])
        send[B + R :] = jnp.where(low, behind[: half - B - R], behind[half:])


def join(level, top, own, parts):
    return pl.pallas_call(
        lambda *refs: join_kernel(level, top, *refs),
        out_shape=(
            jax.ShapeDtypeStruct((PACK, B), jnp.float32),
            jax.ShapeDtypeStruct((B + R if top else PACK // 2, B), jnp.float32),
        ),
        in_specs=[pl.BlockSpec(memory_space=pltpu.VMEM)] * (1 + len(parts)),
        out_specs=[pl.BlockSpec(memory_space=pltpu.VMEM)] * 2,
        compiler_params=pltpu.CompilerParams(vmem_limit_bytes=LIMIT),
        name=f"join{level}",
    )(own, *parts)


def track_kernel(counts, *refs):
    *refs, track = refs
    eye = (
        lax.broadcasted_iota(jnp.int32, (B, B), 0) == lax.broadcasted_iota(jnp.int32, (B, B), 1)
    ).astype(jnp.float32)
    none = jnp.zeros((B + R, B), jnp.float32)
    ahead = jnp.concatenate([eye, none[:R]], axis=0)
    behind = jnp.concatenate([eye, none], axis=0)
    for level, count in enumerate(counts):
        own, parts, refs = refs[0][...], refs[1 : 1 + count], refs[1 + count :]
        first, second = ordered(level, own, partner_pack(parts))
        early, back = turned(first, second)
        left = is_left(level)
        through = mm(back, behind[:B])
        through = jnp.concatenate([through[:B], through[B:] + behind[B:]], axis=0)
        onward = times(early, right_side(ahead[:B]))
        onward = jnp.concatenate([onward[:B], onward[B:] + ahead[B:]], axis=0)
        cross = times(early, right_side(behind[B : 2 * B]))
        cross = jnp.concatenate([behind[:B], cross[:B], cross[B:] + behind[2 * B :]], axis=0)
        ahead = jnp.where(left, ahead, onward)
        behind = jnp.where(left, through, cross)
    track[: B + R] = ahead
    track[B + R :] = behind


def track(steps):
    counts = [len(parts) for _, parts in steps]
    operands = [array for own, parts in steps for array in (own, *parts)]
    return pl.pallas_call(
        lambda *refs: track_kernel(counts, *refs),
        out_shape=jax.ShapeDtypeStruct((PACK, B), jnp.float32),
        in_specs=[pl.BlockSpec(memory_space=pltpu.VMEM)] * len(operands),
        out_specs=pl.BlockSpec(memory_space=pltpu.VMEM),
        compiler_params=pltpu.CompilerParams(vmem_limit_bytes=LIMIT),
        cost_estimate=pl.CostEstimate(
            flops=len(steps) * 2**28, bytes_accessed=len(steps) * 2**19, transcendentals=0
        ),
        name="track",
    )(*operands)


def finish_kernel(level, own, got, track, rows, out):
    left = is_left(level)
    zero = jnp.zeros((R, B), jnp.float32)
    behind = jnp.where(left, zero, got[B:])
    ahead = jnp.where(left, mm(own[B : B + R], got[:B]) + got[B:], zero)
    ahead, behind = left_side(ahead), left_side(behind)
    ahead, behind = (
        times(ahead, right_side(track[B + R : 2 * B + R]))
        + times(behind, right_side(track[2 * B + R : 3 * B + R]))
        + track[3 * B + R :],
        times(behind, right_side(track[:B])) + track[B : B + R],
    )
    ahead, behind = left_side(ahead), left_side(behind)
    for i in range(out.shape[0]):
        out[i] = (
            rows[i, 2 * B :]
            + times(ahead, right_side(rows[i, :B]))
            + times(behind, right_side(rows[i, B : 2 * B]))
        )


def finish(level, own, got, tracked, rows):
    return pl.pallas_call(
        lambda *refs: finish_kernel(level, *refs),
        out_shape=jax.ShapeDtypeStruct((rows.shape[0], R, B), jnp.float32),
        in_specs=[pl.BlockSpec(memory_space=pltpu.VMEM)] * 4,
        out_specs=pl.BlockSpec(memory_space=pltpu.VMEM),
        compiler_params=pltpu.CompilerParams(vmem_limit_bytes=LIMIT),
        name="finish",
    )(own, got, tracked, rows)


def on_device(rhs, pivot_inv, lower_gain, upper_gain):
    devices = lax.axis_size(AXES)
    top = devices.bit_length() - 2
    swap = lambda array, level: lax.ppermute(
        array, AXES, [(i, i ^ (1 << level)) for i in range(devices)]
    )
    inputs = (rhs, pivot_inv, lower_gain, upper_gain)
    pack, rows = local(*(pltpu.with_memory_space_constraint(x, pltpu.HBM) for x in inputs))
    send = pack
    steps = []
    for level in range(top):
        got = swap(send, level)
        parts = (got,) if level == 0 else (got, swap(got, 0))
        steps.append((pack, parts))
        pack, send = join(level, level == top - 1, pack, parts)
    got = swap(send, top)
    return finish(top, pack, got, track(steps), rows)


def solution(mesh):
    placed = P(AXES, None, None)
    return jax.shard_map(
        on_device,
        mesh=mesh,
        in_specs=(placed,) * 4,
        out_specs=placed,
        check_vma=False,
    )
```

```python
import jax
import jax.numpy as jnp
from jax import lax
from jax.experimental import pallas as pl
from jax.experimental.pallas import tpu as pltpu
from jax.sharding import PartitionSpec as P

AXES = ("wide", "narrow")
B = 128
R = 64
PACK = 3 * B + 2 * R
CHUNKS = 3
ORDER = (2, 1, 3)
LIMIT = 12 * 2**20


def halves(value):
    high = value.astype(jnp.bfloat16)
    low = (value - high.astype(jnp.float32)).astype(jnp.bfloat16)
    return high, low


def left_side(value):
    return jnp.concatenate(halves(value), axis=1)


def right_side(value):
    both = jnp.concatenate(halves(value), axis=1)
    return jnp.concatenate([both, both], axis=0)


def times(left, right):
    wide = jnp.dot(left, right, preferred_element_type=jnp.float32)
    return wide[:, :B] + wide[:, B:]


def mm(left, right):
    return times(left_side(left), right_side(right))


def local_kernel(
    rhs_hbm, pivot_hbm, lower_hbm, upper_hbm, pack, rows, rhs, pivot_inv, lower, upper, forward, sems
):
    count = rhs.shape[0]
    pairs = ((pivot_hbm, pivot_inv), (rhs_hbm, rhs), (lower_hbm, lower), (upper_hbm, upper))
    chunk = count // CHUNKS
    copies = {}
    for part in range(CHUNKS):
        for which, (source, target) in enumerate(pairs):
            at = CHUNKS - 1 - part if which == 3 else part
            span = pl.ds(at * chunk, chunk)
            copy = pltpu.make_async_copy(source.at[span], target.at[span], sems.at[which, at])
            copy.start()
            copies[which, at] = copy
    scaled = []
    state = None
    for i in range(count):
        if i % chunk == 0:
            for which in range(3):
                copies[which, i // chunk].wait()
            scaled += [mm(rhs[j], pivot_inv[j]) for j in range(i, i + chunk)]
        if i == 0:
            state = jnp.concatenate([-lower[0], scaled[0]], axis=0)
        else:
            moved = mm(state, lower[i])
            state = jnp.concatenate([-moved[:B], scaled[i] - moved[B:]], axis=0)
        forward[i] = state
    pack[: B + R] = state
    for i in range(count - 1, -1, -1):
        if (i + 1) % chunk == 0:
            copies[3, i // chunk].wait()
        if i == count - 1:
            state = jnp.concatenate([-upper[i], state], axis=0)
        else:
            moved = mm(state, upper[i])
            state = jnp.concatenate([-moved[:B], forward[i] - moved[B:]], axis=0)
        rows[i] = state
    pack[B + R :] = state


def local(rhs, pivot_inv, lower, upper):
    count = rhs.shape[0]
    return pl.pallas_call(
        local_kernel,
        out_shape=(
            jax.ShapeDtypeStruct((PACK, B), jnp.float32),
            jax.ShapeDtypeStruct((count, 2 * B + R, B), jnp.float32),
        ),
        in_specs=[pl.BlockSpec(memory_space=pltpu.HBM)] * 4,
        out_specs=[pl.BlockSpec(memory_space=pltpu.VMEM)] * 2,
        scratch_shapes=[
            pltpu.VMEM(rhs.shape, jnp.float32),
            pltpu.VMEM(pivot_inv.shape, jnp.float32),
            pltpu.VMEM(lower.shape, jnp.float32),
            pltpu.VMEM(upper.shape, jnp.float32),
            pltpu.VMEM((count, B + R, B), jnp.float32),
            pltpu.SemaphoreType.DMA((4, CHUNKS)),
        ],
        compiler_params=pltpu.CompilerParams(vmem_limit_bytes=LIMIT),
        name="local",
    )(rhs, pivot_inv, lower, upper)


def position():
    return lax.axis_index(AXES[0]) * lax.axis_size(AXES[1]) + lax.axis_index(AXES[1])


def is_left(level):
    return (position() >> level) & 1 == 0


def ordered(level, own, other):
    left = is_left(level)
    return jnp.where(left, own, other), jnp.where(left, other, own)


def partner_pack(refs):
    if len(refs) == 1:
        return refs[0][...]
    here, there = refs[0][...], refs[1][...]
    low = position() & 1 == 0
    return jnp.concatenate([jnp.where(low, here, there), jnp.where(low, there, here)], axis=0)


def turned(first, second):
    early = left_side(first[: B + R])
    turn = times(early, right_side(second[2 * B + R : 3 * B + R]))
    back = jnp.concatenate(
        [second[B + R : 2 * B + R], turn[:B], turn[B:] + second[3 * B + R :]], axis=0
    )
    return early, back


def joined(first, second):
    early, back = turned(first, second)
    down = times(early, right_side(second[:B]))
    up = mm(back, first[B + R : 2 * B + R])
    return jnp.concatenate(
        [down[:B], down[B:] + second[B : B + R], up[:B], up[B:] + first[2 * B + R :]], axis=0
    )


def store_half(send, pack):
    half = PACK // 2
    send[...] = jnp.where(position() & 1 == 0, pack[:half], pack[half:])


def pair_kernel(own, other, pack, send):
    value = joined(*ordered(0, own[...], other[...]))
    pack[...] = value
    store_half(send, value)


def quad_kernel(level, top, *refs):
    own, parts, (near, far, pack, send) = refs[0][...], refs[1:7], refs[7:]
    one, two, three = (partner_pack(parts[2 * i : 2 * i + 2]) for i in range(3))
    mine = joined(*ordered(level, own, one))
    theirs = joined(*ordered(level, two, three))
    near[...] = mine
    far[...] = theirs
    value = joined(*ordered(level + 1, mine, theirs))
    pack[...] = value
    if top:
        send[...] = jnp.where(is_left(level + 2), value[: B + R], value[2 * B + R :])
    else:
        store_half(send, value)


def combine(kernel, name, own, parts, extra, send_rows):
    whole = jax.ShapeDtypeStruct((PACK, B), jnp.float32)
    return pl.pallas_call(
        kernel,
        out_shape=(whole,) * (1 + extra) + (jax.ShapeDtypeStruct((send_rows, B), jnp.float32),),
        in_specs=[pl.BlockSpec(memory_space=pltpu.VMEM)] * (1 + len(parts)),
        out_specs=[pl.BlockSpec(memory_space=pltpu.VMEM)] * (2 + extra),
        compiler_params=pltpu.CompilerParams(vmem_limit_bytes=LIMIT),
        name=name,
    )(own, *parts)


def track_kernel(counts, *refs):
    *refs, track = refs
    eye = (
        lax.broadcasted_iota(jnp.int32, (B, B), 0) == lax.broadcasted_iota(jnp.int32, (B, B), 1)
    ).astype(jnp.float32)
    none = jnp.zeros((B + R, B), jnp.float32)
    ahead = jnp.concatenate([eye, none[:R]], axis=0)
    behind = jnp.concatenate([eye, none], axis=0)
    for level, count in enumerate(counts):
        own, parts, refs = refs[0][...], refs[1 : 1 + count], refs[1 + count :]
        first, second = ordered(level, own, partner_pack(parts))
        early, back = turned(first, second)
        left = is_left(level)
        through = mm(back, behind[:B])
        through = jnp.concatenate([through[:B], through[B:] + behind[B:]], axis=0)
        onward = times(early, right_side(ahead[:B]))
        onward = jnp.concatenate([onward[:B], onward[B:] + ahead[B:]], axis=0)
        cross = times(early, right_side(behind[B : 2 * B]))
        cross = jnp.concatenate([behind[:B], cross[:B], cross[B:] + behind[2 * B :]], axis=0)
        ahead = jnp.where(left, ahead, onward)
        behind = jnp.where(left, through, cross)
    track[: B + R] = ahead
    track[B + R :] = behind


def track(steps):
    counts = [len(parts) for _, parts in steps]
    operands = [array for own, parts in steps for array in (own, *parts)]
    return pl.pallas_call(
        lambda *refs: track_kernel(counts, *refs),
        out_shape=jax.ShapeDtypeStruct((PACK, B), jnp.float32),
        in_specs=[pl.BlockSpec(memory_space=pltpu.VMEM)] * len(operands),
        out_specs=pl.BlockSpec(memory_space=pltpu.VMEM),
        compiler_params=pltpu.CompilerParams(vmem_limit_bytes=LIMIT),
        cost_estimate=pl.CostEstimate(
            flops=len(steps) * 2**28, bytes_accessed=len(steps) * 2**19, transcendentals=0
        ),
        name="track",
    )(*operands)


def finish_kernel(level, own, got, track, rows, out):
    left = is_left(level)
    zero = jnp.zeros((R, B), jnp.float32)
    behind = jnp.where(left, zero, got[B:])
    ahead = jnp.where(left, mm(own[B : B + R], got[:B]) + got[B:], zero)
    ahead, behind = left_side(ahead), left_side(behind)
    ahead, behind = (
        times(ahead, right_side(track[B + R : 2 * B + R]))
        + times(behind, right_side(track[2 * B + R : 3 * B + R]))
        + track[3 * B + R :],
        times(behind, right_side(track[:B])) + track[B : B + R],
    )
    ahead, behind = left_side(ahead), left_side(behind)
    for i in range(out.shape[0]):
        out[i] = (
            rows[i, 2 * B :]
            + times(ahead, right_side(rows[i, :B]))
            + times(behind, right_side(rows[i, B : 2 * B]))
        )


def finish(level, own, got, tracked, rows):
    return pl.pallas_call(
        lambda *refs: finish_kernel(level, *refs),
        out_shape=jax.ShapeDtypeStruct((rows.shape[0], R, B), jnp.float32),
        in_specs=[pl.BlockSpec(memory_space=pltpu.VMEM)] * 4,
        out_specs=pl.BlockSpec(memory_space=pltpu.VMEM),
        compiler_params=pltpu.CompilerParams(vmem_limit_bytes=LIMIT),
        name="finish",
    )(own, got, tracked, rows)


def on_device(rhs, pivot_inv, lower_gain, upper_gain):
    devices = lax.axis_size(AXES)
    top = devices.bit_length() - 2
    plane = devices >> 3
    swap = lambda array, bits: lax.ppermute(array, AXES, [(i, i ^ bits) for i in range(devices)])
    inputs = (rhs, pivot_inv, lower_gain, upper_gain)
    pack, rows = local(*(pltpu.with_memory_space_constraint(x, pltpu.HBM) for x in inputs))
    other = swap(pack, 1)
    steps = [(pack, (other,))]
    pack, send = combine(pair_kernel, "pair", pack, (other,), 0, PACK // 2)
    for level in range(1, top, 2):
        last = level == top - 2
        got = {bits: swap(send, bits << level) for bits in ORDER}
        twin = {bits: swap(got[bits], 1) for bits in ORDER}
        parts = [part for bits in (1, 2, 3) for part in (got[bits], twin[bits])]
        steps.append((pack, tuple(parts[:2])))
        near, far, pack, send = combine(
            lambda *refs, level=level, last=last: quad_kernel(level, last, *refs),
            f"quad{level}",
            pack,
            parts,
            2,
            B + R if last else PACK // 2,
        )
        steps.append((near, (far,)))
    mirror = [(i, devices - plane - i + 2 * (i % plane)) for i in range(devices)]
    got = lax.ppermute(send, AXES, mirror)
    return finish(top, pack, got, track(steps), rows)


def solution(mesh):
    placed = P(AXES, None, None)
    return jax.shard_map(
        on_device,
        mesh=mesh,
        in_specs=(placed,) * 4,
        out_specs=placed,
        check_vma=False,
    )
```

```python
import jax
import jax.numpy as jnp
from jax import lax
from jax.experimental import pallas as pl
from jax.experimental.pallas import tpu as pltpu
from jax.sharding import PartitionSpec as P

AXES = ("wide", "narrow")
B = 128
R = 64
PACK = 3 * B + 2 * R
PARTS = 2
OUT_ROWS = 3
PLANS = ((1, (1, 2)), (3, (1, 2)), (5, (1, 3)))
LIMIT = 12 * 2**20


def halves(value):
    high = value.astype(jnp.bfloat16)
    low = (value - high.astype(jnp.float32)).astype(jnp.bfloat16)
    return high, low


def left_side(value):
    return jnp.concatenate(halves(value), axis=1)


def right_side(value):
    both = jnp.concatenate(halves(value), axis=1)
    return jnp.concatenate([both, both], axis=0)


def times(left, right):
    wide = jnp.dot(left, right, preferred_element_type=jnp.float32)
    return wide[:, :B] + wide[:, B:]


def mm(left, right):
    return times(left_side(left), right_side(right))


def local_kernel(
    rhs_hbm,
    pivot_hbm,
    lower_hbm,
    upper_hbm,
    pack,
    parts,
    rows,
    rhs,
    pivot_inv,
    lower,
    upper,
    forward,
    sems,
):
    count = rhs.shape[1]
    pairs = ((pivot_hbm, pivot_inv), (rhs_hbm, rhs), (lower_hbm, lower), (upper_hbm, upper))
    edges = (0, 1, count // 2, count)
    spans = list(zip(edges[:-1], edges[1:]))
    waits = {}

    def fetch(which, slot, start, stop, row):
        source, target = pairs[which]
        span = (slice(None), pl.ds(start, stop - start))
        copy = pltpu.make_async_copy(source.at[span], target.at[span], sems.at[which, slot])
        copy.start()
        waits.setdefault((which // 3, row), []).append(copy)

    for slot, (start, stop) in enumerate(spans):
        for which in range(3):
            fetch(which, slot, start, stop, start)
    fetch(3, 1, count // 2, count, count - 1)
    fetch(3, 0, 0, count // 2, count // 2 - 1)
    states = [None] * PARTS
    scaled = {}
    for i in range(count):
        if (0, i) in waits:
            for copy in waits[0, i]:
                copy.wait()
            stop = next(stop for start, stop in spans if start == i)
            for j in range(i, stop):
                for part in range(PARTS):
                    scaled[part, j] = mm(rhs[part, j], pivot_inv[part, j])
        for part in range(PARTS):
            if i == 0:
                state = jnp.concatenate([-lower[part, 0], scaled[part, 0]], axis=0)
            else:
                moved = mm(states[part], lower[part, i])
                state = jnp.concatenate([-moved[:B], scaled[part, i] - moved[B:]], axis=0)
            forward[part, i] = state
            states[part] = state
    for part in range(PARTS):
        parts[part, : B + R] = states[part]
    for i in range(count - 1, -1, -1):
        for copy in waits.get((1, i), []):
            copy.wait()
        for part in range(PARTS):
            if i == count - 1:
                state = jnp.concatenate([-upper[part, i], states[part]], axis=0)
            else:
                moved = mm(states[part], upper[part, i])
                state = jnp.concatenate([-moved[:B], forward[part, i] - moved[B:]], axis=0)
            rows[part, i] = state
            states[part] = state
    for part in range(PARTS):
        parts[part, B + R :] = states[part]
    pack[...] = joined(parts[0], parts[1])


def local(rhs, pivot_inv, lower, upper):
    inputs = [
        pltpu.with_memory_space_constraint(
            x.reshape((PARTS, x.shape[0] // PARTS) + x.shape[1:]), pltpu.HBM
        )
        for x in (rhs, pivot_inv, lower, upper)
    ]
    count = inputs[0].shape[1]
    return pl.pallas_call(
        local_kernel,
        out_shape=(
            jax.ShapeDtypeStruct((PACK, B), jnp.float32),
            jax.ShapeDtypeStruct((PARTS, PACK, B), jnp.float32),
            jax.ShapeDtypeStruct((PARTS, count, 2 * B + R, B), jnp.float32),
        ),
        in_specs=[pl.BlockSpec(memory_space=pltpu.HBM)] * 4,
        out_specs=[pl.BlockSpec(memory_space=pltpu.VMEM)] * 3,
        scratch_shapes=[pltpu.VMEM(x.shape, jnp.float32) for x in inputs]
        + [
            pltpu.VMEM((PARTS, count, B + R, B), jnp.float32),
            pltpu.SemaphoreType.DMA((4, 3)),
        ],
        compiler_params=pltpu.CompilerParams(vmem_limit_bytes=LIMIT),
        name="local",
    )(*inputs)


def position():
    return lax.axis_index(AXES[0]) * lax.axis_size(AXES[1]) + lax.axis_index(AXES[1])


def is_left(level):
    return (position() >> level) & 1 == 0


def ordered(level, own, other):
    left = is_left(level)
    return jnp.where(left, own, other), jnp.where(left, other, own)


def by_core(here, there):
    low = position() & 1 == 0
    return jnp.where(low, here, there), jnp.where(low, there, here)


def turned(first, second):
    early = left_side(first[: B + R])
    turn = times(early, right_side(second[2 * B + R : 3 * B + R]))
    back = jnp.concatenate(
        [second[B + R : 2 * B + R], turn[:B], turn[B:] + second[3 * B + R :]], axis=0
    )
    return early, back


def joined(first, second):
    early, back = turned(first, second)
    down = times(early, right_side(second[:B]))
    up = mm(back, first[B + R : 2 * B + R])
    return jnp.concatenate(
        [down[:B], down[B:] + second[B : B + R], up[:B], up[B:] + first[2 * B + R :]], axis=0
    )


def store_half(send, pack):
    half = PACK // 2
    send[...] = jnp.where(position() & 1 == 0, pack[:half], pack[half:])


def pair_kernel(own, other, pack, send):
    value = joined(*ordered(0, own[...], other[...]))
    pack[...] = value
    store_half(send, value)


def quad_kernel(level, plan, top, *refs):
    own, whole, whole_twin, half, half_twin, one, near, far, pack, send = refs
    partner = dict(zip(plan, by_core(whole[...], whole_twin[...])))
    partner[6 - sum(plan)] = jnp.concatenate(by_core(half[...], half_twin[...]), axis=0)
    one[...] = partner[1]
    mine = joined(*ordered(level, own[...], partner[1]))
    theirs = joined(*ordered(level, partner[2], partner[3]))
    near[...] = mine
    far[...] = theirs
    value = joined(*ordered(level + 1, mine, theirs))
    pack[...] = value
    if top:
        send[...] = jnp.where(is_left(level + 2), value[: B + R], value[2 * B + R :])
    else:
        store_half(send, value)


def combine(kernel, name, own, parts, extra, send_rows):
    whole = jax.ShapeDtypeStruct((PACK, B), jnp.float32)
    return pl.pallas_call(
        kernel,
        out_shape=(whole,) * (1 + extra) + (jax.ShapeDtypeStruct((send_rows, B), jnp.float32),),
        in_specs=[pl.BlockSpec(memory_space=pltpu.VMEM)] * (1 + len(parts)),
        out_specs=[pl.BlockSpec(memory_space=pltpu.VMEM)] * (2 + extra),
        compiler_params=pltpu.CompilerParams(vmem_limit_bytes=LIMIT),
        name=name,
    )(own, *parts)


def track_kernel(levels, *refs):
    parts, track = refs[0], refs[-1]
    eye = (
        lax.broadcasted_iota(jnp.int32, (B, B), 0) == lax.broadcasted_iota(jnp.int32, (B, B), 1)
    ).astype(jnp.float32)
    none = jnp.zeros((B + R, B), jnp.float32)
    _, back = turned(parts[0], parts[1])
    aheads = [jnp.concatenate([eye, none[:R]], axis=0), parts[0, : B + R]]
    behinds = [back, jnp.concatenate([eye, none], axis=0)]
    for level in range(levels):
        first, second = ordered(level, refs[1 + 2 * level][...], refs[2 + 2 * level][...])
        early, back = turned(first, second)
        late = left_side(back)
        left = is_left(level)
        for part in range(PARTS):
            ahead, behind = aheads[part], behinds[part]
            through = times(late, right_side(behind[:B]))
            through = jnp.concatenate([through[:B], through[B:] + behind[B:]], axis=0)
            onward = times(early, right_side(ahead[:B]))
            onward = jnp.concatenate([onward[:B], onward[B:] + ahead[B:]], axis=0)
            cross = times(early, right_side(behind[B : 2 * B]))
            cross = jnp.concatenate([behind[:B], cross[:B], cross[B:] + behind[2 * B :]], axis=0)
            aheads[part] = jnp.where(left, ahead, onward)
            behinds[part] = jnp.where(left, through, cross)
    for part in range(PARTS):
        track[part, : B + R] = aheads[part]
        track[part, B + R :] = behinds[part]


def track(parts, steps):
    return pl.pallas_call(
        lambda *refs: track_kernel(len(steps), *refs),
        out_shape=jax.ShapeDtypeStruct((PARTS, PACK, B), jnp.float32),
        in_specs=[pl.BlockSpec(memory_space=pltpu.VMEM)] * (1 + 2 * len(steps)),
        out_specs=pl.BlockSpec(memory_space=pltpu.VMEM),
        compiler_params=pltpu.CompilerParams(vmem_limit_bytes=LIMIT),
        cost_estimate=pl.CostEstimate(
            flops=len(steps) * 2**28, bytes_accessed=len(steps) * 2**19, transcendentals=0
        ),
        name="track",
    )(parts, *(array for step in steps for array in step))


def finish_kernel(level, own, got, track, rows, out_hbm, out, sems):
    left = is_left(level)
    zero = jnp.zeros((R, B), jnp.float32)
    behind = jnp.where(left, zero, got[B:])
    ahead = jnp.where(left, mm(own[B : B + R], got[:B]) + got[B:], zero)
    ahead, behind = left_side(ahead), left_side(behind)
    count = rows.shape[1]
    copies = []
    for part in range(PARTS):
        x_in = (
            times(ahead, right_side(track[part, B + R : 2 * B + R]))
            + times(behind, right_side(track[part, 2 * B + R : 3 * B + R]))
            + track[part, 3 * B + R :]
        )
        f_in = times(behind, right_side(track[part, :B])) + track[part, B : B + R]
        x_in, f_in = left_side(x_in), left_side(f_in)
        for i in range(count):
            out[part * count + i] = (
                rows[part, i, 2 * B :]
                + times(x_in, right_side(rows[part, i, :B]))
                + times(f_in, right_side(rows[part, i, B : 2 * B]))
            )
            done = part * count + i + 1
            if done % OUT_ROWS == 0:
                span = pl.ds(done - OUT_ROWS, OUT_ROWS)
                copies.append(
                    pltpu.make_async_copy(out.at[span], out_hbm.at[span], sems.at[len(copies)])
                )
                copies[-1].start()
    for copy in copies:
        copy.wait()


def finish(level, own, got, tracked, rows):
    shape = (rows.shape[0] * rows.shape[1], R, B)
    return pl.pallas_call(
        lambda *refs: finish_kernel(level, *refs),
        out_shape=jax.ShapeDtypeStruct(shape, jnp.float32),
        in_specs=[pl.BlockSpec(memory_space=pltpu.VMEM)] * 4,
        out_specs=pl.BlockSpec(memory_space=pltpu.HBM),
        scratch_shapes=[
            pltpu.VMEM(shape, jnp.float32),
            pltpu.SemaphoreType.DMA((shape[0] // OUT_ROWS,)),
        ],
        compiler_params=pltpu.CompilerParams(vmem_limit_bytes=LIMIT),
        name="finish",
    )(own, got, tracked, rows)


def on_device(rhs, pivot_inv, lower_gain, upper_gain):
    devices = lax.axis_size(AXES)
    top = devices.bit_length() - 2
    plane = devices >> 3
    swap = lambda array, even, odd: lax.ppermute(
        array, AXES, [(i, i ^ (odd if i & 1 else even)) for i in range(devices)]
    )
    pack, parts, rows = local(rhs, pivot_inv, lower_gain, upper_gain)
    other = swap(pack, 1, 1)
    steps = [(pack, other)]
    pack, half = combine(pair_kernel, "pair", pack, (other,), 0, PACK // 2)
    for level, plan in PLANS:
        last = level == top - 2
        third = 6 - sum(plan)
        halves = swap(half, third << level, third << level)
        whole = swap(pack, plan[0] << level, plan[1] << level)
        received = (whole, swap(whole, 1, 1), halves, swap(halves, 1, 1))
        own = pack
        one, near, far, pack, half = combine(
            lambda *refs, level=level, plan=plan, last=last: quad_kernel(level, plan, last, *refs),
            f"quad{level}",
            own,
            received,
            3,
            B + R if last else PACK // 2,
        )
        steps += [(own, one), (near, far)]
    mirror = [(i, devices - plane - i + 2 * (i % plane)) for i in range(devices)]
    got = lax.ppermute(half, AXES, mirror)
    return finish(top, pack, got, track(parts, steps), rows)


def solution(mesh):
    placed = P(AXES, None, None)
    return jax.shard_map(
        on_device,
        mesh=mesh,
        in_specs=(placed,) * 4,
        out_specs=placed,
        check_vma=False,
    )
```

```python
import jax
import jax.numpy as jnp
from jax import lax
from jax.experimental import pallas as pl
from jax.experimental.pallas import tpu as pltpu
from jax.sharding import PartitionSpec as P

AXES = ("wide", "narrow")
B = 128
R = 64
PACK = 3 * B + 2 * R
PARTS = 2
OUT_ROWS = 3
FACING = (6, 7, 4, 5, 2, 3, 0, 1)
PLANS = ((1, (1, 2)), (3, (1, 2)), (5, (1, 3)))
LIMIT = 12 * 2**20


def halves(value):
    high = value.astype(jnp.bfloat16)
    low = (value - high.astype(jnp.float32)).astype(jnp.bfloat16)
    return high, low


def left_side(value):
    return jnp.concatenate(halves(value), axis=1)


def right_side(value):
    both = jnp.concatenate(halves(value), axis=1)
    return jnp.concatenate([both, both], axis=0)


def times(left, right):
    wide = jnp.dot(left, right, preferred_element_type=jnp.float32)
    return wide[:, :B] + wide[:, B:]


def mm(left, right):
    return times(left_side(left), right_side(right))


def local_kernel(
    rhs_hbm,
    pivot_hbm,
    lower_hbm,
    upper_hbm,
    pack,
    parts,
    rows,
    rhs,
    pivot_inv,
    lower,
    upper,
    forward,
    sems,
):
    count = rhs.shape[1]
    pairs = ((pivot_hbm, pivot_inv), (rhs_hbm, rhs), (lower_hbm, lower), (upper_hbm, upper))
    edges = (0, 1, count // 2, count)
    spans = list(zip(edges[:-1], edges[1:]))
    waits = {}

    def fetch(which, slot, start, stop, row):
        source, target = pairs[which]
        span = (slice(None), pl.ds(start, stop - start))
        copy = pltpu.make_async_copy(source.at[span], target.at[span], sems.at[which, slot])
        copy.start()
        waits.setdefault((which // 3, row), []).append(copy)

    for slot, (start, stop) in enumerate(spans):
        for which in range(3):
            fetch(which, slot, start, stop, start)
    fetch(3, 1, count // 2, count, count - 1)
    fetch(3, 0, 0, count // 2, count // 2 - 1)
    states = [None] * PARTS
    scaled = {}
    for i in range(count):
        if (0, i) in waits:
            for copy in waits[0, i]:
                copy.wait()
            stop = next(stop for start, stop in spans if start == i)
            for j in range(i, stop):
                for part in range(PARTS):
                    scaled[part, j] = mm(rhs[part, j], pivot_inv[part, j])
        for part in range(PARTS):
            if i == 0:
                state = jnp.concatenate([-lower[part, 0], scaled[part, 0]], axis=0)
            else:
                moved = mm(states[part], lower[part, i])
                state = jnp.concatenate([-moved[:B], scaled[part, i] - moved[B:]], axis=0)
            forward[part, i] = state
            states[part] = state
    for part in range(PARTS):
        parts[part, : B + R] = states[part]
    for i in range(count - 1, -1, -1):
        for copy in waits.get((1, i), []):
            copy.wait()
        for part in range(PARTS):
            if i == count - 1:
                state = jnp.concatenate([-upper[part, i], states[part]], axis=0)
            else:
                moved = mm(states[part], upper[part, i])
                state = jnp.concatenate([-moved[:B], forward[part, i] - moved[B:]], axis=0)
            rows[part, i] = state
            states[part] = state
    for part in range(PARTS):
        parts[part, B + R :] = states[part]
    pack[...] = joined(parts[0], parts[1])


def local(rhs, pivot_inv, lower, upper):
    inputs = [
        pltpu.with_memory_space_constraint(
            x.reshape((PARTS, x.shape[0] // PARTS) + x.shape[1:]), pltpu.HBM
        )
        for x in (rhs, pivot_inv, lower, upper)
    ]
    count = inputs[0].shape[1]
    return pl.pallas_call(
        local_kernel,
        out_shape=(
            jax.ShapeDtypeStruct((PACK, B), jnp.float32),
            jax.ShapeDtypeStruct((PARTS, PACK, B), jnp.float32),
            jax.ShapeDtypeStruct((PARTS, count, 2 * B + R, B), jnp.float32),
        ),
        in_specs=[pl.BlockSpec(memory_space=pltpu.HBM)] * 4,
        out_specs=[pl.BlockSpec(memory_space=pltpu.VMEM)] * 3,
        scratch_shapes=[pltpu.VMEM(x.shape, jnp.float32) for x in inputs]
        + [
            pltpu.VMEM((PARTS, count, B + R, B), jnp.float32),
            pltpu.SemaphoreType.DMA((4, 3)),
        ],
        compiler_params=pltpu.CompilerParams(vmem_limit_bytes=LIMIT),
        name="local",
    )(*inputs)


def position():
    return lax.axis_index(AXES[0]) * lax.axis_size(AXES[1]) + lax.axis_index(AXES[1])


def is_left(level):
    return (position() >> level) & 1 == 0


def ordered(level, own, other):
    left = is_left(level)
    return jnp.where(left, own, other), jnp.where(left, other, own)


def by_core(here, there):
    low = position() & 1 == 0
    return jnp.where(low, here, there), jnp.where(low, there, here)


def turned(first, second):
    early = left_side(first[: B + R])
    turn = times(early, right_side(second[2 * B + R : 3 * B + R]))
    back = jnp.concatenate(
        [second[B + R : 2 * B + R], turn[:B], turn[B:] + second[3 * B + R :]], axis=0
    )
    return early, back


def joined(first, second):
    early, back = turned(first, second)
    down = times(early, right_side(second[:B]))
    up = mm(back, first[B + R : 2 * B + R])
    return jnp.concatenate(
        [down[:B], down[B:] + second[B : B + R], up[:B], up[B:] + first[2 * B + R :]], axis=0
    )


def store_half(send, pack):
    half = PACK // 2
    send[...] = jnp.where(position() & 1 == 0, pack[:half], pack[half:])


def pair_kernel(own, other, pack, send):
    value = joined(*ordered(0, own[...], other[...]))
    pack[...] = value
    store_half(send, value)


def quad_kernel(level, plan, top, *refs):
    own, whole, whole_twin, half, half_twin, one, near, far, pack, send = refs
    partner = dict(zip(plan, by_core(whole[...], whole_twin[...])))
    partner[6 - sum(plan)] = jnp.concatenate(by_core(half[...], half_twin[...]), axis=0)
    one[...] = partner[1]
    mine = joined(*ordered(level, own[...], partner[1]))
    theirs = joined(*ordered(level, partner[2], partner[3]))
    near[...] = mine
    far[...] = theirs
    value = joined(*ordered(level + 1, mine, theirs))
    pack[...] = value
    if top:
        send[...] = jnp.where(is_left(level + 2), value[: B + R], value[2 * B + R :])
    else:
        store_half(send, value)


def combine(kernel, name, own, parts, extra, send_rows):
    whole = jax.ShapeDtypeStruct((PACK, B), jnp.float32)
    return pl.pallas_call(
        kernel,
        out_shape=(whole,) * (1 + extra) + (jax.ShapeDtypeStruct((send_rows, B), jnp.float32),),
        in_specs=[pl.BlockSpec(memory_space=pltpu.VMEM)] * (1 + len(parts)),
        out_specs=[pl.BlockSpec(memory_space=pltpu.VMEM)] * (2 + extra),
        compiler_params=pltpu.CompilerParams(vmem_limit_bytes=LIMIT),
        name=name,
    )(own, *parts)


def advanced(level, first, second, aheads, behinds):
    early, back = turned(first, second)
    late = left_side(back)
    left = is_left(level)
    for part in range(PARTS):
        ahead, behind = aheads[part], behinds[part]
        through = times(late, right_side(behind[:B]))
        through = jnp.concatenate([through[:B], through[B:] + behind[B:]], axis=0)
        onward = times(early, right_side(ahead[:B]))
        onward = jnp.concatenate([onward[:B], onward[B:] + ahead[B:]], axis=0)
        cross = times(early, right_side(behind[B : 2 * B]))
        cross = jnp.concatenate([behind[:B], cross[:B], cross[B:] + behind[2 * B :]], axis=0)
        aheads[part] = jnp.where(left, ahead, onward)
        behinds[part] = jnp.where(left, through, cross)


def prepare_kernel(levels, *refs):
    parts, rows, pairs, (track, spread) = refs[0], refs[1], refs[2:-2], refs[-2:]
    eye = (
        lax.broadcasted_iota(jnp.int32, (B, B), 0) == lax.broadcasted_iota(jnp.int32, (B, B), 1)
    ).astype(jnp.float32)
    none = jnp.zeros((B + R, B), jnp.float32)
    _, back = turned(parts[0], parts[1])
    aheads = [jnp.concatenate([eye, none[:R]], axis=0), parts[0, : B + R]]
    behinds = [back, jnp.concatenate([eye, none], axis=0)]
    for level in range(levels):
        first, second = ordered(level, pairs[2 * level][...], pairs[2 * level + 1][...])
        advanced(level, first, second, aheads, behinds)
    for part in range(PARTS):
        track[part, : B + R] = aheads[part]
        track[part, B + R :] = behinds[part]
        for i in range(rows.shape[1]):
            spread[part, i] = left_side(rows[part, i, : 2 * B])


def prepare(parts, rows, steps):
    return pl.pallas_call(
        lambda *refs: prepare_kernel(len(steps), *refs),
        out_shape=(
            jax.ShapeDtypeStruct((PARTS, PACK, B), jnp.float32),
            jax.ShapeDtypeStruct(rows.shape[:2] + (2 * B, 2 * B), jnp.bfloat16),
        ),
        in_specs=[pl.BlockSpec(memory_space=pltpu.VMEM)] * (2 + 2 * len(steps)),
        out_specs=[pl.BlockSpec(memory_space=pltpu.VMEM)] * 2,
        compiler_params=pltpu.CompilerParams(vmem_limit_bytes=LIMIT),
        cost_estimate=pl.CostEstimate(flops=2**31, bytes_accessed=2**23, transcendentals=0),
        name="prepare",
    )(parts, rows, *(array for step in steps for array in step))


def refine_kernel(start, top, *refs):
    track, pairs, (weights, offsets) = refs[0], refs[1:-2], refs[-2:]
    aheads = [track[part, : B + R] for part in range(PARTS)]
    behinds = [track[part, B + R :] for part in range(PARTS)]
    for i in range(len(pairs) // 2):
        first, second = ordered(start + i, pairs[2 * i][...], pairs[2 * i + 1][...])
        advanced(start + i, first, second, aheads, behinds)
    left = is_left(top)
    for part in range(PARTS):
        ahead, behind = aheads[part], behinds[part]
        weights[part, 0] = right_side(jnp.where(left, behind[:B], behind[B : 2 * B]))
        weights[part, 1] = right_side(jnp.where(left, 0.0, ahead[:B]))
        offsets[part, 0] = behind[2 * B :]
        offsets[part, 1] = ahead[B:]


def refine(start, top, tracked, steps):
    return pl.pallas_call(
        lambda *refs: refine_kernel(start, top, *refs),
        out_shape=(
            jax.ShapeDtypeStruct((PARTS, 2, 2 * B, 2 * B), jnp.bfloat16),
            jax.ShapeDtypeStruct((PARTS, 2, R, B), jnp.float32),
        ),
        in_specs=[pl.BlockSpec(memory_space=pltpu.VMEM)] * (1 + 2 * len(steps)),
        out_specs=[pl.BlockSpec(memory_space=pltpu.VMEM)] * 2,
        compiler_params=pltpu.CompilerParams(vmem_limit_bytes=LIMIT),
        cost_estimate=pl.CostEstimate(flops=2**30, bytes_accessed=2**22, transcendentals=0),
        name="refine",
    )(tracked, *(array for step in steps for array in step))


def finish_kernel(level, own, got, weights, offsets, spread, rows, out_hbm, out, sems):
    carry = jnp.where(is_left(level), mm(own[B : B + R], got[:B]), 0.0) + got[B:]
    carry = left_side(carry)
    count = rows.shape[1]
    copies = []
    for part in range(PARTS):
        both = jnp.concatenate(
            [times(carry, weights[part, i]) + offsets[part, i] for i in range(2)], axis=1
        )
        both = jnp.concatenate(halves(both), axis=0)
        for i in range(count):
            wide = jnp.dot(both, spread[part, i], preferred_element_type=jnp.float32)
            wide = wide[:R] + wide[R:]
            out[part * count + i] = rows[part, i, 2 * B :] + wide[:, :B] + wide[:, B:]
            done = part * count + i + 1
            if done % OUT_ROWS == 0:
                span = pl.ds(done - OUT_ROWS, OUT_ROWS)
                copies.append(
                    pltpu.make_async_copy(out.at[span], out_hbm.at[span], sems.at[len(copies)])
                )
                copies[-1].start()
    for copy in copies:
        copy.wait()


def finish(level, own, got, weights, offsets, spread, rows):
    shape = (rows.shape[0] * rows.shape[1], R, B)
    return pl.pallas_call(
        lambda *refs: finish_kernel(level, *refs),
        out_shape=jax.ShapeDtypeStruct(shape, jnp.float32),
        in_specs=[pl.BlockSpec(memory_space=pltpu.VMEM)] * 6,
        out_specs=pl.BlockSpec(memory_space=pltpu.HBM),
        scratch_shapes=[
            pltpu.VMEM(shape, jnp.float32),
            pltpu.SemaphoreType.DMA((shape[0] // OUT_ROWS,)),
        ],
        compiler_params=pltpu.CompilerParams(vmem_limit_bytes=LIMIT),
        name="finish",
    )(own, got, weights, offsets, spread, rows)


def on_device(rhs, pivot_inv, lower_gain, upper_gain):
    devices = lax.axis_size(AXES)
    top = devices.bit_length() - 2
    plane = devices >> 3
    swap = lambda array, even, odd: lax.ppermute(
        array, AXES, [(i, i ^ (odd if i & 1 else even)) for i in range(devices)]
    )
    pack, parts, rows = local(rhs, pivot_inv, lower_gain, upper_gain)
    other = swap(pack, 1, 1)
    steps = [(pack, other)]
    pack, half = combine(pair_kernel, "pair", pack, (other,), 0, PACK // 2)
    for level, plan in PLANS:
        last = level == top - 2
        third = 6 - sum(plan)
        halves = swap(half, third << level, third << level)
        whole = swap(pack, plan[0] << level, plan[1] << level)
        if last:
            aside = prepare(parts, rows, steps)
            whole, aside = lax.optimization_barrier((whole, aside))
        received = (whole, swap(whole, 1, 1), halves, swap(halves, 1, 1))
        own = pack
        one, near, far, pack, half = combine(
            lambda *refs, level=level, plan=plan, last=last: quad_kernel(level, plan, last, *refs),
            f"quad{level}",
            own,
            received,
            3,
            B + R if last else PACK // 2,
        )
        steps += [(own, one), (near, far)]
    facing = [(i, FACING[i // plane] * plane + i % plane) for i in range(devices)]
    got = lax.ppermute(half, AXES, facing)
    tracked, spread = aside
    weights, offsets = refine(top - 2, top, tracked, steps[top - 2 :])
    return finish(top, pack, got, weights, offsets, spread, rows)


def solution(mesh):
    placed = P(AXES, None, None)
    return jax.shard_map(
        on_device,
        mesh=mesh,
        in_specs=(placed,) * 4,
        out_specs=placed,
        check_vma=False,
    )
```

```python
import jax
import jax.numpy as jnp
from jax import lax
from jax.experimental import pallas as pl
from jax.experimental.pallas import tpu as pltpu
from jax.sharding import PartitionSpec as P

AXES = ("wide", "narrow")
B = 128
R = 64
PACK = 3 * B + 2 * R
PARTS = 2
OUT_ROWS = 3
FACING = (6, 7, 4, 5, 2, 3, 0, 1)
ROUNDS = (1, 3, 5)
LIMIT = 12 * 2**20


def halves(value):
    high = value.astype(jnp.bfloat16)
    low = (value - high.astype(jnp.float32)).astype(jnp.bfloat16)
    return high, low


def left_side(value):
    return jnp.concatenate(halves(value), axis=1)


def right_side(value):
    both = jnp.concatenate(halves(value), axis=1)
    return jnp.concatenate([both, both], axis=0)


def times(left, right):
    wide = jnp.dot(left, right, preferred_element_type=jnp.float32)
    return wide[:, :B] + wide[:, B:]


def mm(left, right):
    return times(left_side(left), right_side(right))


def local_kernel(
    rhs_hbm,
    pivot_hbm,
    lower_hbm,
    upper_hbm,
    pack,
    parts,
    rows,
    rhs,
    pivot_inv,
    lower,
    upper,
    forward,
    sems,
):
    count = rhs.shape[1]
    pairs = ((pivot_hbm, pivot_inv), (rhs_hbm, rhs), (lower_hbm, lower), (upper_hbm, upper))
    edges = (0, 1, count // 2, count)
    spans = list(zip(edges[:-1], edges[1:]))
    waits = {}

    def fetch(which, slot, start, stop, row):
        source, target = pairs[which]
        span = (slice(None), pl.ds(start, stop - start))
        copy = pltpu.make_async_copy(source.at[span], target.at[span], sems.at[which, slot])
        copy.start()
        waits.setdefault((which // 3, row), []).append(copy)

    for slot, (start, stop) in enumerate(spans):
        for which in range(3):
            fetch(which, slot, start, stop, start)
    fetch(3, 1, count // 2, count, count - 1)
    fetch(3, 0, 0, count // 2, count // 2 - 1)
    states = [None] * PARTS
    scaled = {}
    for i in range(count):
        if (0, i) in waits:
            for copy in waits[0, i]:
                copy.wait()
            stop = next(stop for start, stop in spans if start == i)
            for j in range(i, stop):
                for part in range(PARTS):
                    scaled[part, j] = mm(rhs[part, j], pivot_inv[part, j])
        for part in range(PARTS):
            if i == 0:
                state = jnp.concatenate([-lower[part, 0], scaled[part, 0]], axis=0)
            else:
                moved = mm(states[part], lower[part, i])
                state = jnp.concatenate([-moved[:B], scaled[part, i] - moved[B:]], axis=0)
            forward[part, i] = state
            states[part] = state
    for part in range(PARTS):
        parts[part, : B + R] = states[part]
    for i in range(count - 1, -1, -1):
        for copy in waits.get((1, i), []):
            copy.wait()
        for part in range(PARTS):
            if i == count - 1:
                state = jnp.concatenate([-upper[part, i], states[part]], axis=0)
            else:
                moved = mm(states[part], upper[part, i])
                state = jnp.concatenate([-moved[:B], forward[part, i] - moved[B:]], axis=0)
            rows[part, i] = state
            states[part] = state
    for part in range(PARTS):
        parts[part, B + R :] = states[part]
    pack[...] = joined(parts[0], parts[1])


def local(rhs, pivot_inv, lower, upper):
    inputs = [
        pltpu.with_memory_space_constraint(
            x.reshape((PARTS, x.shape[0] // PARTS) + x.shape[1:]), pltpu.HBM
        )
        for x in (rhs, pivot_inv, lower, upper)
    ]
    count = inputs[0].shape[1]
    return pl.pallas_call(
        local_kernel,
        out_shape=(
            jax.ShapeDtypeStruct((PACK, B), jnp.float32),
            jax.ShapeDtypeStruct((PARTS, PACK, B), jnp.float32),
            jax.ShapeDtypeStruct((PARTS, count, 2 * B + R, B), jnp.float32),
        ),
        in_specs=[pl.BlockSpec(memory_space=pltpu.HBM)] * 4,
        out_specs=[pl.BlockSpec(memory_space=pltpu.VMEM)] * 3,
        scratch_shapes=[pltpu.VMEM(x.shape, jnp.float32) for x in inputs]
        + [
            pltpu.VMEM((PARTS, count, B + R, B), jnp.float32),
            pltpu.SemaphoreType.DMA((4, 3)),
        ],
        compiler_params=pltpu.CompilerParams(vmem_limit_bytes=LIMIT),
        name="local",
    )(*inputs)


def position():
    return lax.axis_index(AXES[0]) * lax.axis_size(AXES[1]) + lax.axis_index(AXES[1])


def is_left(level):
    return (position() >> level) & 1 == 0


def ordered(level, own, other):
    left = is_left(level)
    return jnp.where(left, own, other), jnp.where(left, other, own)


def by_core(here, there):
    low = position() & 1 == 0
    return jnp.where(low, here, there), jnp.where(low, there, here)


def turned(first, second):
    early = left_side(first[: B + R])
    turn = times(early, right_side(second[2 * B + R : 3 * B + R]))
    back = jnp.concatenate(
        [second[B + R : 2 * B + R], turn[:B], turn[B:] + second[3 * B + R :]], axis=0
    )
    return early, back


def joined(first, second):
    early, back = turned(first, second)
    down = times(early, right_side(second[:B]))
    up = mm(back, first[B + R : 2 * B + R])
    return jnp.concatenate(
        [down[:B], down[B:] + second[B : B + R], up[:B], up[B:] + first[2 * B + R :]], axis=0
    )


def store_half(send, pack):
    half = PACK // 2
    send[...] = jnp.where(position() & 1 == 0, pack[:half], pack[half:])


def pair_kernel(own, other, pack, send):
    value = joined(*ordered(0, own[...], other[...]))
    pack[...] = value
    store_half(send, value)


def quad_kernel(level, top, own, *refs):
    gots, (twin, one, near, far, pack, send) = refs[:3], refs[3:]
    half = PACK // 2
    partners = [
        jnp.concatenate(by_core(got[...], twin[i * half : (i + 1) * half]), axis=0)
        for i, got in enumerate(gots)
    ]
    one[...] = partners[0]
    mine = joined(*ordered(level, own[...], partners[0]))
    theirs = joined(*ordered(level, partners[1], partners[2]))
    near[...] = mine
    far[...] = theirs
    value = joined(*ordered(level + 1, mine, theirs))
    pack[...] = value
    if top:
        send[...] = jnp.where(is_left(level + 2), value[: B + R], value[2 * B + R :])
    else:
        store_half(send, value)


def combine(kernel, name, own, parts, extra, send_rows):
    whole = jax.ShapeDtypeStruct((PACK, B), jnp.float32)
    return pl.pallas_call(
        kernel,
        out_shape=(whole,) * (1 + extra) + (jax.ShapeDtypeStruct((send_rows, B), jnp.float32),),
        in_specs=[pl.BlockSpec(memory_space=pltpu.VMEM)] * (1 + len(parts)),
        out_specs=[pl.BlockSpec(memory_space=pltpu.VMEM)] * (2 + extra),
        compiler_params=pltpu.CompilerParams(vmem_limit_bytes=LIMIT),
        name=name,
    )(own, *parts)


def advanced(level, first, second, aheads, behinds):
    early, back = turned(first, second)
    late = left_side(back)
    left = is_left(level)
    for part in range(PARTS):
        ahead, behind = aheads[part], behinds[part]
        through = times(late, right_side(behind[:B]))
        through = jnp.concatenate([through[:B], through[B:] + behind[B:]], axis=0)
        onward = times(early, right_side(ahead[:B]))
        onward = jnp.concatenate([onward[:B], onward[B:] + ahead[B:]], axis=0)
        cross = times(early, right_side(behind[B : 2 * B]))
        cross = jnp.concatenate([behind[:B], cross[:B], cross[B:] + behind[2 * B :]], axis=0)
        aheads[part] = jnp.where(left, ahead, onward)
        behinds[part] = jnp.where(left, through, cross)


def prepare_kernel(levels, *refs):
    parts, rows, pairs, (track, spread) = refs[0], refs[1], refs[2:-2], refs[-2:]
    eye = (
        lax.broadcasted_iota(jnp.int32, (B, B), 0) == lax.broadcasted_iota(jnp.int32, (B, B), 1)
    ).astype(jnp.float32)
    none = jnp.zeros((B + R, B), jnp.float32)
    _, back = turned(parts[0], parts[1])
    aheads = [jnp.concatenate([eye, none[:R]], axis=0), parts[0, : B + R]]
    behinds = [back, jnp.concatenate([eye, none], axis=0)]
    for level in range(levels):
        first, second = ordered(level, pairs[2 * level][...], pairs[2 * level + 1][...])
        advanced(level, first, second, aheads, behinds)
    for part in range(PARTS):
        track[part, : B + R] = aheads[part]
        track[part, B + R :] = behinds[part]
        for i in range(rows.shape[1]):
            spread[part, i] = left_side(rows[part, i, : 2 * B])


def prepare(parts, rows, steps):
    return pl.pallas_call(
        lambda *refs: prepare_kernel(len(steps), *refs),
        out_shape=(
            jax.ShapeDtypeStruct((PARTS, PACK, B), jnp.float32),
            jax.ShapeDtypeStruct(rows.shape[:2] + (2 * B, 2 * B), jnp.bfloat16),
        ),
        in_specs=[pl.BlockSpec(memory_space=pltpu.VMEM)] * (2 + 2 * len(steps)),
        out_specs=[pl.BlockSpec(memory_space=pltpu.VMEM)] * 2,
        compiler_params=pltpu.CompilerParams(vmem_limit_bytes=LIMIT),
        cost_estimate=pl.CostEstimate(flops=2**31, bytes_accessed=2**23, transcendentals=0),
        name="prepare",
    )(parts, rows, *(array for step in steps for array in step))


def refine_kernel(start, top, *refs):
    track, pairs, (weights, offsets) = refs[0], refs[1:-2], refs[-2:]
    aheads = [track[part, : B + R] for part in range(PARTS)]
    behinds = [track[part, B + R :] for part in range(PARTS)]
    for i in range(len(pairs) // 2):
        first, second = ordered(start + i, pairs[2 * i][...], pairs[2 * i + 1][...])
        advanced(start + i, first, second, aheads, behinds)
    left = is_left(top)
    for part in range(PARTS):
        ahead, behind = aheads[part], behinds[part]
        weights[part, 0] = right_side(jnp.where(left, behind[:B], behind[B : 2 * B]))
        weights[part, 1] = right_side(jnp.where(left, 0.0, ahead[:B]))
        offsets[part, 0] = behind[2 * B :]
        offsets[part, 1] = ahead[B:]


def refine(start, top, tracked, steps):
    return pl.pallas_call(
        lambda *refs: refine_kernel(start, top, *refs),
        out_shape=(
            jax.ShapeDtypeStruct((PARTS, 2, 2 * B, 2 * B), jnp.bfloat16),
            jax.ShapeDtypeStruct((PARTS, 2, R, B), jnp.float32),
        ),
        in_specs=[pl.BlockSpec(memory_space=pltpu.VMEM)] * (1 + 2 * len(steps)),
        out_specs=[pl.BlockSpec(memory_space=pltpu.VMEM)] * 2,
        compiler_params=pltpu.CompilerParams(vmem_limit_bytes=LIMIT),
        cost_estimate=pl.CostEstimate(flops=2**30, bytes_accessed=2**22, transcendentals=0),
        name="refine",
    )(tracked, *(array for step in steps for array in step))


def finish_kernel(level, own, got, weights, offsets, spread, rows, out_hbm, out, sems):
    carry = jnp.where(is_left(level), mm(own[B : B + R], got[:B]), 0.0) + got[B:]
    carry = left_side(carry)
    count = rows.shape[1]
    copies = []
    for part in range(PARTS):
        both = jnp.concatenate(
            [times(carry, weights[part, i]) + offsets[part, i] for i in range(2)], axis=1
        )
        both = jnp.concatenate(halves(both), axis=0)
        for i in range(count):
            wide = jnp.dot(both, spread[part, i], preferred_element_type=jnp.float32)
            wide = wide[:R] + wide[R:]
            out[part * count + i] = rows[part, i, 2 * B :] + wide[:, :B] + wide[:, B:]
            done = part * count + i + 1
            if done % OUT_ROWS == 0:
                span = pl.ds(done - OUT_ROWS, OUT_ROWS)
                copies.append(
                    pltpu.make_async_copy(out.at[span], out_hbm.at[span], sems.at[len(copies)])
                )
                copies[-1].start()
    for copy in copies:
        copy.wait()


def finish(level, own, got, weights, offsets, spread, rows):
    shape = (rows.shape[0] * rows.shape[1], R, B)
    return pl.pallas_call(
        lambda *refs: finish_kernel(level, *refs),
        out_shape=jax.ShapeDtypeStruct(shape, jnp.float32),
        in_specs=[pl.BlockSpec(memory_space=pltpu.VMEM)] * 6,
        out_specs=pl.BlockSpec(memory_space=pltpu.HBM),
        scratch_shapes=[
            pltpu.VMEM(shape, jnp.float32),
            pltpu.SemaphoreType.DMA((shape[0] // OUT_ROWS,)),
        ],
        compiler_params=pltpu.CompilerParams(vmem_limit_bytes=LIMIT),
        name="finish",
    )(own, got, weights, offsets, spread, rows)


def on_device(rhs, pivot_inv, lower_gain, upper_gain):
    devices = lax.axis_size(AXES)
    top = devices.bit_length() - 2
    plane = devices >> 3
    swap = lambda array, bits: lax.ppermute(array, AXES, [(i, i ^ bits) for i in range(devices)])
    pack, parts, rows = local(rhs, pivot_inv, lower_gain, upper_gain)
    other = swap(pack, 1)
    steps = [(pack, other)]
    pack, half = combine(pair_kernel, "pair", pack, (other,), 0, PACK // 2)
    for level in ROUNDS:
        last = level == top - 2
        gots = tuple(swap(half, bits << level) for bits in (1, 2, 3))
        if last:
            aside = prepare(parts, rows, steps)
            gots, aside = lax.optimization_barrier((gots, aside))
        received = gots + (swap(jnp.concatenate(gots, axis=0), 1),)
        own = pack
        one, near, far, pack, half = combine(
            lambda *refs, level=level, last=last: quad_kernel(level, last, *refs),
            f"quad{level}",
            own,
            received,
            3,
            B + R if last else PACK // 2,
        )
        steps += [(own, one), (near, far)]
    facing = [(i, FACING[i // plane] * plane + i % plane) for i in range(devices)]
    got = lax.ppermute(half, AXES, facing)
    tracked, spread = aside
    weights, offsets = refine(top - 2, top, tracked, steps[top - 2 :])
    return finish(top, pack, got, weights, offsets, spread, rows)


def solution(mesh):
    placed = P(AXES, None, None)
    return jax.shard_map(
        on_device,
        mesh=mesh,
        in_specs=(placed,) * 4,
        out_specs=placed,
        check_vma=False,
    )
```

```python
import jax
import jax.numpy as jnp
from jax import lax
from jax.experimental import pallas as pl
from jax.experimental.pallas import tpu as pltpu
from jax.sharding import PartitionSpec as P

AXES = ("wide", "narrow")
B = 128
R = 64
PACK = 3 * B + 2 * R
PARTS = 2
OUT_ROWS = 3
PLANS = ((1, (1, 2)), (3, (1, 2)))
TOP = {(z, c): ((6, 7, 4, 5)[z], c) for z in range(4) for c in range(2)}
TOP |= {(4, 0): (1, 0), (4, 1): (2, 1), (5, 0): (0, 0), (5, 1): (3, 1)}
LIMIT = 12 * 2**20


def halves(value):
    high = value.astype(jnp.bfloat16)
    low = (value - high.astype(jnp.float32)).astype(jnp.bfloat16)
    return high, low


def left_side(value):
    return jnp.concatenate(halves(value), axis=1)


def right_side(value):
    both = jnp.concatenate(halves(value), axis=1)
    return jnp.concatenate([both, both], axis=0)


def times(left, right):
    wide = jnp.dot(left, right, preferred_element_type=jnp.float32)
    return wide[:, :B] + wide[:, B:]


def mm(left, right):
    return times(left_side(left), right_side(right))


def local_kernel(
    rhs_hbm,
    pivot_hbm,
    lower_hbm,
    upper_hbm,
    pack,
    parts,
    rows,
    rhs,
    pivot_inv,
    lower,
    upper,
    forward,
    sems,
):
    count = rhs.shape[1]
    pairs = ((pivot_hbm, pivot_inv), (rhs_hbm, rhs), (lower_hbm, lower), (upper_hbm, upper))
    edges = (0, count // 3, count)
    spans = list(zip(edges[:-1], edges[1:]))
    waits = {}

    def fetch(which, slot, start, stop, row):
        source, target = pairs[which]
        span = (slice(None), pl.ds(start, stop - start))
        copy = pltpu.make_async_copy(source.at[span], target.at[span], sems.at[which, slot])
        copy.start()
        waits.setdefault((which // 3, row), []).append(copy)

    for slot, (start, stop) in enumerate(spans):
        for which in range(3):
            fetch(which, slot, start, stop, start)
    fetch(3, 0, 0, count, count - 1)
    states = [None] * PARTS
    scaled = {}
    for i in range(count):
        if (0, i) in waits:
            for copy in waits[0, i]:
                copy.wait()
            stop = next(stop for start, stop in spans if start == i)
            for j in range(i, stop):
                for part in range(PARTS):
                    scaled[part, j] = mm(rhs[part, j], pivot_inv[part, j])
        for part in range(PARTS):
            if i == 0:
                state = jnp.concatenate([-lower[part, 0], scaled[part, 0]], axis=0)
            else:
                moved = mm(states[part], lower[part, i])
                state = jnp.concatenate([-moved[:B], scaled[part, i] - moved[B:]], axis=0)
            forward[part, i] = state
            states[part] = state
    for part in range(PARTS):
        parts[part, : B + R] = states[part]
    for i in range(count - 1, -1, -1):
        for copy in waits.get((1, i), []):
            copy.wait()
        for part in range(PARTS):
            if i == count - 1:
                state = jnp.concatenate([-upper[part, i], states[part]], axis=0)
            else:
                moved = mm(states[part], upper[part, i])
                state = jnp.concatenate([-moved[:B], forward[part, i] - moved[B:]], axis=0)
            rows[part, i] = state
            states[part] = state
    for part in range(PARTS):
        parts[part, B + R :] = states[part]
    pack[...] = joined(parts[0], parts[1])


def local(rhs, pivot_inv, lower, upper):
    inputs = [
        pltpu.with_memory_space_constraint(
            x.reshape((PARTS, x.shape[0] // PARTS) + x.shape[1:]), pltpu.HBM
        )
        for x in (rhs, pivot_inv, lower, upper)
    ]
    count = inputs[0].shape[1]
    return pl.pallas_call(
        local_kernel,
        out_shape=(
            jax.ShapeDtypeStruct((PACK, B), jnp.float32),
            jax.ShapeDtypeStruct((PARTS, PACK, B), jnp.float32),
            jax.ShapeDtypeStruct((PARTS, count, 2 * B + R, B), jnp.float32),
        ),
        in_specs=[pl.BlockSpec(memory_space=pltpu.HBM)] * 4,
        out_specs=[pl.BlockSpec(memory_space=pltpu.VMEM)] * 3,
        scratch_shapes=[pltpu.VMEM(x.shape, jnp.float32) for x in inputs]
        + [
            pltpu.VMEM((PARTS, count, B + R, B), jnp.float32),
            pltpu.SemaphoreType.DMA((4, 2)),
        ],
        compiler_params=pltpu.CompilerParams(vmem_limit_bytes=LIMIT),
        name="local",
    )(*inputs)


def position():
    return lax.axis_index(AXES[0]) * lax.axis_size(AXES[1]) + lax.axis_index(AXES[1])


def is_left(level):
    return (position() >> level) & 1 == 0


def ordered(level, own, other):
    left = is_left(level)
    return jnp.where(left, own, other), jnp.where(left, other, own)


def by_core(here, there):
    low = position() & 1 == 0
    return jnp.where(low, here, there), jnp.where(low, there, here)


def turned(first, second):
    early = left_side(first[: B + R])
    turn = times(early, right_side(second[2 * B + R : 3 * B + R]))
    back = jnp.concatenate(
        [second[B + R : 2 * B + R], turn[:B], turn[B:] + second[3 * B + R :]], axis=0
    )
    return early, back


def joined(first, second):
    early, back = turned(first, second)
    down = times(early, right_side(second[:B]))
    up = mm(back, first[B + R : 2 * B + R])
    return jnp.concatenate(
        [down[:B], down[B:] + second[B : B + R], up[:B], up[B:] + first[2 * B + R :]], axis=0
    )


def store_half(send, pack):
    half = PACK // 2
    send[...] = jnp.where(position() & 1 == 0, pack[:half], pack[half:])


def pair_kernel(own, other, pack, send):
    value = joined(*ordered(0, own[...], other[...]))
    pack[...] = value
    store_half(send, value)


def quad_kernel(level, plan, own, whole, whole_twin, half, half_twin, one, near, far, pack, send):
    partner = dict(zip(plan, by_core(whole[...], whole_twin[...])))
    partner[6 - sum(plan)] = jnp.concatenate(by_core(half[...], half_twin[...]), axis=0)
    one[...] = partner[1]
    mine = joined(*ordered(level, own[...], partner[1]))
    theirs = joined(*ordered(level, partner[2], partner[3]))
    near[...] = mine
    far[...] = theirs
    value = joined(*ordered(level + 1, mine, theirs))
    pack[...] = value
    store_half(send, value)


def planes_kernel(level, own, half, half_twin, other, pack, rest, send):
    other[...] = jnp.concatenate(by_core(half[...], half_twin[...]), axis=0)
    value = joined(*ordered(level, own[...], other[...]))
    pack[...] = value
    rest[...] = value[B + R :]
    send[...] = jnp.where(position() >> (level + 1) == 3, value[2 * B + R :], value[: B + R])


def meet_kernel(level, own, got, send):
    pair = position() >> level
    gain, shift = own[:B], own[B : B + R]
    second = pair == 1
    moved = mm(
        jnp.where(second, got[...], own[: B + R]), jnp.where(second, gain, got[:B])
    )
    moved = jnp.concatenate([moved[:B], moved[B:] + jnp.where(second, shift, got[B:])], axis=0)
    back = mm(moved, own[B + R : 2 * B + R]) + own[2 * B + R :]
    send[...] = jnp.where(pair < 2, moved, back)


def combine(kernel, name, own, parts, *out_rows):
    return pl.pallas_call(
        kernel,
        out_shape=tuple(jax.ShapeDtypeStruct((rows, B), jnp.float32) for rows in out_rows),
        in_specs=[pl.BlockSpec(memory_space=pltpu.VMEM)] * (1 + len(parts)),
        out_specs=[pl.BlockSpec(memory_space=pltpu.VMEM)] * len(out_rows),
        compiler_params=pltpu.CompilerParams(vmem_limit_bytes=LIMIT),
        name=name,
    )(own, *parts)


def advanced(level, first, second, aheads, behinds):
    early, back = turned(first, second)
    late = left_side(back)
    left = is_left(level)
    for part in range(PARTS):
        ahead, behind = aheads[part], behinds[part]
        through = times(late, right_side(behind[:B]))
        through = jnp.concatenate([through[:B], through[B:] + behind[B:]], axis=0)
        onward = times(early, right_side(ahead[:B]))
        onward = jnp.concatenate([onward[:B], onward[B:] + ahead[B:]], axis=0)
        cross = times(early, right_side(behind[B : 2 * B]))
        cross = jnp.concatenate([behind[:B], cross[:B], cross[B:] + behind[2 * B :]], axis=0)
        aheads[part] = jnp.where(left, ahead, onward)
        behinds[part] = jnp.where(left, through, cross)


def prepare_kernel(levels, *refs):
    parts, rows, pairs, (track, spread) = refs[0], refs[1], refs[2:-2], refs[-2:]
    eye = (
        lax.broadcasted_iota(jnp.int32, (B, B), 0) == lax.broadcasted_iota(jnp.int32, (B, B), 1)
    ).astype(jnp.float32)
    none = jnp.zeros((B + R, B), jnp.float32)
    _, back = turned(parts[0], parts[1])
    aheads = [jnp.concatenate([eye, none[:R]], axis=0), parts[0, : B + R]]
    behinds = [back, jnp.concatenate([eye, none], axis=0)]
    for level in range(levels):
        first, second = ordered(level, pairs[2 * level][...], pairs[2 * level + 1][...])
        advanced(level, first, second, aheads, behinds)
    for part in range(PARTS):
        track[part, : B + R] = aheads[part]
        track[part, B + R :] = behinds[part]
        for i in range(rows.shape[1]):
            spread[part, i] = left_side(rows[part, i, : 2 * B])


def prepare(parts, rows, steps):
    return pl.pallas_call(
        lambda *refs: prepare_kernel(len(steps), *refs),
        out_shape=(
            jax.ShapeDtypeStruct((PARTS, PACK, B), jnp.float32),
            jax.ShapeDtypeStruct(rows.shape[:2] + (2 * B, 2 * B), jnp.bfloat16),
        ),
        in_specs=[pl.BlockSpec(memory_space=pltpu.VMEM)] * (2 + 2 * len(steps)),
        out_specs=[pl.BlockSpec(memory_space=pltpu.VMEM)] * 2,
        compiler_params=pltpu.CompilerParams(vmem_limit_bytes=LIMIT),
        cost_estimate=pl.CostEstimate(flops=2**31, bytes_accessed=2**23, transcendentals=0),
        name="prepare",
    )(parts, rows, *(array for step in steps for array in step))


def refine_kernel(level, track, own, got, rest, weights, offsets):
    pair = position() >> level
    eye = (
        lax.broadcasted_iota(jnp.int32, (B, B), 0) == lax.broadcasted_iota(jnp.int32, (B, B), 1)
    ).astype(jnp.float32)
    unit = jnp.concatenate([eye, jnp.zeros((R, B), jnp.float32)], axis=0)
    first = pair == 0
    turn = mm(own[: B + R], jnp.where(first, rest[B : 2 * B], got[:B]))
    turn = jnp.concatenate(
        [
            jnp.where(first, rest[:B], turn[:B]),
            turn[B:] + jnp.where(first, rest[2 * B :], got[B:]),
        ],
        axis=0,
    )
    x_map = jnp.where(pair == 1, unit, jnp.where(pair == 3, 0.0, turn))
    earlier = jnp.concatenate([jnp.where(pair == 1, 0.0, got[:B]), got[B:]], axis=0)
    f_map = jnp.where(first, 0.0, jnp.where(pair == 2, unit, earlier))
    x_left, f_left = left_side(x_map), left_side(f_map)
    for part in range(PARTS):
        ahead, behind = track[part, : B + R], track[part, B + R :]
        x_out = times(x_left, right_side(behind[:B])) + times(
            f_left, right_side(behind[B : 2 * B])
        )
        f_out = times(f_left, right_side(ahead[:B]))
        weights[part, 0] = right_side(x_out[:B])
        weights[part, 1] = right_side(f_out[:B])
        offsets[part, 0] = x_out[B:] + behind[2 * B :]
        offsets[part, 1] = f_out[B:] + ahead[B:]


def refine(level, tracked, own, got, rest):
    return pl.pallas_call(
        lambda *refs: refine_kernel(level, *refs),
        out_shape=(
            jax.ShapeDtypeStruct((PARTS, 2, 2 * B, 2 * B), jnp.bfloat16),
            jax.ShapeDtypeStruct((PARTS, 2, R, B), jnp.float32),
        ),
        in_specs=[pl.BlockSpec(memory_space=pltpu.VMEM)] * 4,
        out_specs=[pl.BlockSpec(memory_space=pltpu.VMEM)] * 2,
        compiler_params=pltpu.CompilerParams(vmem_limit_bytes=LIMIT),
        cost_estimate=pl.CostEstimate(flops=2**30, bytes_accessed=2**22, transcendentals=0),
        name="refine",
    )(tracked, own, got, rest)


def finish_kernel(level, own, here, twin, weights, offsets, spread, rows, out_hbm, out, sems):
    left = is_left(level)
    other_core = (position() & 1) != ((position() >> (level - 1)) & 1)
    got = jnp.where(jnp.logical_and(left, other_core), twin[...], here[...])
    carry = jnp.where(left, mm(own[B:], got[:B]), 0.0) + got[B:]
    carry = left_side(carry)
    count = rows.shape[1]
    copies = []
    for part in range(PARTS):
        both = jnp.concatenate(
            [times(carry, weights[part, i]) + offsets[part, i] for i in range(2)], axis=1
        )
        both = jnp.concatenate(halves(both), axis=0)
        for i in range(count):
            wide = jnp.dot(both, spread[part, i], preferred_element_type=jnp.float32)
            wide = wide[:R] + wide[R:]
            out[part * count + i] = rows[part, i, 2 * B :] + wide[:, :B] + wide[:, B:]
            done = part * count + i + 1
            if done % OUT_ROWS == 0:
                span = pl.ds(done - OUT_ROWS, OUT_ROWS)
                copies.append(
                    pltpu.make_async_copy(out.at[span], out_hbm.at[span], sems.at[len(copies)])
                )
                copies[-1].start()
    for copy in copies:
        copy.wait()


def finish(level, own, here, twin, weights, offsets, spread, rows):
    shape = (rows.shape[0] * rows.shape[1], R, B)
    return pl.pallas_call(
        lambda *refs: finish_kernel(level, *refs),
        out_shape=jax.ShapeDtypeStruct(shape, jnp.float32),
        in_specs=[pl.BlockSpec(memory_space=pltpu.VMEM)] * 7,
        out_specs=pl.BlockSpec(memory_space=pltpu.HBM),
        scratch_shapes=[
            pltpu.VMEM(shape, jnp.float32),
            pltpu.SemaphoreType.DMA((shape[0] // OUT_ROWS,)),
        ],
        compiler_params=pltpu.CompilerParams(vmem_limit_bytes=LIMIT),
        name="finish",
    )(own, here, twin, weights, offsets, spread, rows)


def on_device(rhs, pivot_inv, lower_gain, upper_gain):
    devices = lax.axis_size(AXES)
    plane = devices // 8

    def send(array, pairs):
        return lax.ppermute(array, AXES, pairs)

    def swap(array, even, odd):
        return send(array, [(i, i ^ (odd if i & 1 else even)) for i in range(devices)])

    def at(i, z, core):
        return z * plane + i % plane // 2 * 2 + core

    pack, parts, rows = local(rhs, pivot_inv, lower_gain, upper_gain)
    other = swap(pack, 1, 1)
    steps = [(pack, other)]
    pack, half = combine(pair_kernel, "pair", pack, (other,), PACK, PACK // 2)
    for level, plan in PLANS:
        third = 6 - sum(plan)
        whole = swap(pack, plan[0] << level, plan[1] << level)
        halves_got = swap(half, third << level, third << level)
        received = (whole, swap(whole, 1, 1), halves_got, swap(halves_got, 1, 1))
        own = pack
        one, near, far, pack, half = combine(
            lambda *refs, level=level, plan=plan: quad_kernel(level, plan, *refs),
            f"quad{level}",
            own,
            received,
            *(PACK,) * 4,
            PACK // 2,
        )
        steps += [(own, one), (near, far)]
    level = 5
    half = swap(half, 1 << level, 1 << level)
    own = pack
    other, pack, rest, edge = combine(
        lambda *refs: planes_kernel(level, *refs),
        "planes",
        own,
        (half, swap(half, 1, 1)),
        PACK,
        PACK,
        PACK - B - R,
        B + R,
    )
    steps.append((own, other))
    bit = 2 * plane
    got = swap(edge, bit, bit)
    rest = send(rest, [(i, i ^ bit) for i in range(devices) if i // bit == 1])
    aside = prepare(parts, rows, steps)
    got, aside = lax.optimization_barrier((got, aside))
    (edge,) = combine(
        lambda *refs: meet_kernel(level + 1, *refs), "meet", pack, (got,), B + R
    )
    target = {i: TOP.get((i // plane, i & 1)) for i in range(devices)}
    here = send(edge, [(i, at(i, *goal)) for i, goal in target.items() if goal])
    tracked, spread = aside
    maps = refine(level + 1, tracked, pack, got, rest)
    here, maps = lax.optimization_barrier((here, maps))
    chips = range(0, plane, 2)
    twin = send(here, [(at(i, z, z // 2), at(i, z, 1 - z // 2)) for z in range(4) for i in chips])
    return finish(level + 2, edge, here, twin, *maps, spread, rows)


def solution(mesh):
    placed = P(AXES, None, None)
    return jax.shard_map(
        on_device,
        mesh=mesh,
        in_specs=(placed,) * 4,
        out_specs=placed,
        check_vma=False,
    )
```

```python
import jax
import jax.numpy as jnp
from jax import lax
from jax.experimental import pallas as pl
from jax.experimental.pallas import tpu as pltpu
from jax.sharding import PartitionSpec as P

AXES = ("wide", "narrow")
B = 128
R = 64
PACK = 3 * B + 2 * R
PARTS = 2
OUT_ROWS = 3
FACING = (6, 7, 4, 5, 2, 3, 0, 1)
PLANS = ((1, (1, 2)), (3, (1, 2)), (5, (1, 3)))
LIMIT = 12 * 2**20


def halves(value):
    high = value.astype(jnp.bfloat16)
    low = (value - high.astype(jnp.float32)).astype(jnp.bfloat16)
    return high, low


def left_side(value):
    return jnp.concatenate(halves(value), axis=1)


def right_side(value):
    both = jnp.concatenate(halves(value), axis=1)
    return jnp.concatenate([both, both], axis=0)


def times(left, right):
    wide = jnp.dot(left, right, preferred_element_type=jnp.float32)
    return wide[:, :B] + wide[:, B:]


def mm(left, right):
    return times(left_side(left), right_side(right))


def local_kernel(
    rhs_hbm,
    pivot_hbm,
    lower_hbm,
    upper_hbm,
    pack,
    parts,
    rows,
    rhs,
    pivot_inv,
    lower,
    upper,
    forward,
    sems,
):
    count = rhs.shape[1]
    pairs = ((pivot_hbm, pivot_inv), (rhs_hbm, rhs), (lower_hbm, lower), (upper_hbm, upper))
    edges = (0, count // 3, count)
    spans = list(zip(edges[:-1], edges[1:]))
    waits = {}

    def fetch(which, slot, start, stop, row):
        source, target = pairs[which]
        span = (slice(None), pl.ds(start, stop - start))
        copy = pltpu.make_async_copy(source.at[span], target.at[span], sems.at[which, slot])
        copy.start()
        waits.setdefault((which // 3, row), []).append(copy)

    for slot, (start, stop) in enumerate(spans):
        for which in range(3):
            fetch(which, slot, start, stop, start)
    fetch(3, 0, 0, count, count - 1)
    states = [None] * PARTS
    scaled = {}
    for i in range(count):
        if (0, i) in waits:
            for copy in waits[0, i]:
                copy.wait()
            stop = next(stop for start, stop in spans if start == i)
            for j in range(i, stop):
                for part in range(PARTS):
                    scaled[part, j] = mm(rhs[part, j], pivot_inv[part, j])
        for part in range(PARTS):
            if i == 0:
                state = jnp.concatenate([-lower[part, 0], scaled[part, 0]], axis=0)
            else:
                moved = mm(states[part], lower[part, i])
                state = jnp.concatenate([-moved[:B], scaled[part, i] - moved[B:]], axis=0)
            forward[part, i] = state
            states[part] = state
    for part in range(PARTS):
        parts[part, : B + R] = states[part]
    for i in range(count - 1, -1, -1):
        for copy in waits.get((1, i), []):
            copy.wait()
        for part in range(PARTS):
            if i == count - 1:
                state = jnp.concatenate([-upper[part, i], states[part]], axis=0)
            else:
                moved = mm(states[part], upper[part, i])
                state = jnp.concatenate([-moved[:B], forward[part, i] - moved[B:]], axis=0)
            rows[part, i] = state
            states[part] = state
    for part in range(PARTS):
        parts[part, B + R :] = states[part]
    pack[...] = joined(parts[0], parts[1])


def local(rhs, pivot_inv, lower, upper):
    inputs = [
        pltpu.with_memory_space_constraint(
            x.reshape((PARTS, x.shape[0] // PARTS) + x.shape[1:]), pltpu.HBM
        )
        for x in (rhs, pivot_inv, lower, upper)
    ]
    count = inputs[0].shape[1]
    return pl.pallas_call(
        local_kernel,
        out_shape=(
            jax.ShapeDtypeStruct((PACK, B), jnp.float32),
            jax.ShapeDtypeStruct((PARTS, PACK, B), jnp.float32),
            jax.ShapeDtypeStruct((PARTS, count, 2 * B + R, B), jnp.float32),
        ),
        in_specs=[pl.BlockSpec(memory_space=pltpu.HBM)] * 4,
        out_specs=[pl.BlockSpec(memory_space=pltpu.VMEM)] * 3,
        scratch_shapes=[pltpu.VMEM(x.shape, jnp.float32) for x in inputs]
        + [
            pltpu.VMEM((PARTS, count, B + R, B), jnp.float32),
            pltpu.SemaphoreType.DMA((4, 2)),
        ],
        compiler_params=pltpu.CompilerParams(vmem_limit_bytes=LIMIT),
        name="local",
    )(*inputs)


def position():
    return lax.axis_index(AXES[0]) * lax.axis_size(AXES[1]) + lax.axis_index(AXES[1])


def is_left(level):
    return (position() >> level) & 1 == 0


def ordered(level, own, other):
    left = is_left(level)
    return jnp.where(left, own, other), jnp.where(left, other, own)


def by_core(here, there):
    low = position() & 1 == 0
    return jnp.where(low, here, there), jnp.where(low, there, here)


def turned(first, second):
    early = left_side(first[: B + R])
    turn = times(early, right_side(second[2 * B + R : 3 * B + R]))
    back = jnp.concatenate(
        [second[B + R : 2 * B + R], turn[:B], turn[B:] + second[3 * B + R :]], axis=0
    )
    return early, back


def joined(first, second):
    early, back = turned(first, second)
    down = times(early, right_side(second[:B]))
    up = mm(back, first[B + R : 2 * B + R])
    return jnp.concatenate(
        [down[:B], down[B:] + second[B : B + R], up[:B], up[B:] + first[2 * B + R :]], axis=0
    )


def store_half(send, pack):
    half = pack.shape[0] // 2
    send[...] = jnp.where(position() & 1 == 0, pack[:half], pack[half:])


def pair_kernel(own, other, pack, send):
    value = joined(*ordered(0, own[...], other[...]))
    pack[...] = value
    store_half(send, value)


def quad_kernel(level, plan, top, *refs):
    own, whole, whole_twin, half, half_twin, one, near, far, pack, send = refs
    partner = dict(zip(plan, by_core(whole[...], whole_twin[...])))
    partner[6 - sum(plan)] = jnp.concatenate(by_core(half[...], half_twin[...]), axis=0)
    one[...] = partner[1]
    mine = joined(*ordered(level, own[...], partner[1]))
    theirs = joined(*ordered(level, partner[2], partner[3]))
    near[...] = mine
    far[...] = theirs
    value = joined(*ordered(level + 1, mine, theirs))
    pack[...] = value
    if top:
        store_half(send, jnp.where(is_left(level + 2), value[: B + R], value[2 * B + R :]))
    else:
        store_half(send, value)


def combine(kernel, name, own, parts, extra, send_rows):
    whole = jax.ShapeDtypeStruct((PACK, B), jnp.float32)
    return pl.pallas_call(
        kernel,
        out_shape=(whole,) * (1 + extra) + (jax.ShapeDtypeStruct((send_rows, B), jnp.float32),),
        in_specs=[pl.BlockSpec(memory_space=pltpu.VMEM)] * (1 + len(parts)),
        out_specs=[pl.BlockSpec(memory_space=pltpu.VMEM)] * (2 + extra),
        compiler_params=pltpu.CompilerParams(vmem_limit_bytes=LIMIT),
        name=name,
    )(own, *parts)


def advanced(level, first, second, aheads, behinds):
    early, back = turned(first, second)
    late = left_side(back)
    left = is_left(level)
    for part in range(PARTS):
        ahead, behind = aheads[part], behinds[part]
        through = times(late, right_side(behind[:B]))
        through = jnp.concatenate([through[:B], through[B:] + behind[B:]], axis=0)
        onward = times(early, right_side(ahead[:B]))
        onward = jnp.concatenate([onward[:B], onward[B:] + ahead[B:]], axis=0)
        cross = times(early, right_side(behind[B : 2 * B]))
        cross = jnp.concatenate([behind[:B], cross[:B], cross[B:] + behind[2 * B :]], axis=0)
        aheads[part] = jnp.where(left, ahead, onward)
        behinds[part] = jnp.where(left, through, cross)


def prepare_kernel(levels, *refs):
    parts, rows, pairs, (track, spread) = refs[0], refs[1], refs[2:-2], refs[-2:]
    eye = (
        lax.broadcasted_iota(jnp.int32, (B, B), 0) == lax.broadcasted_iota(jnp.int32, (B, B), 1)
    ).astype(jnp.float32)
    none = jnp.zeros((B + R, B), jnp.float32)
    _, back = turned(parts[0], parts[1])
    aheads = [jnp.concatenate([eye, none[:R]], axis=0), parts[0, : B + R]]
    behinds = [back, jnp.concatenate([eye, none], axis=0)]
    for level in range(levels):
        first, second = ordered(level, pairs[2 * level][...], pairs[2 * level + 1][...])
        advanced(level, first, second, aheads, behinds)
    for part in range(PARTS):
        track[part, : B + R] = aheads[part]
        track[part, B + R :] = behinds[part]
        for i in range(rows.shape[1]):
            spread[part, i] = left_side(rows[part, i, : 2 * B])


def prepare(parts, rows, steps):
    return pl.pallas_call(
        lambda *refs: prepare_kernel(len(steps), *refs),
        out_shape=(
            jax.ShapeDtypeStruct((PARTS, PACK, B), jnp.float32),
            jax.ShapeDtypeStruct(rows.shape[:2] + (2 * B, 2 * B), jnp.bfloat16),
        ),
        in_specs=[pl.BlockSpec(memory_space=pltpu.VMEM)] * (2 + 2 * len(steps)),
        out_specs=[pl.BlockSpec(memory_space=pltpu.VMEM)] * 2,
        compiler_params=pltpu.CompilerParams(vmem_limit_bytes=LIMIT),
        cost_estimate=pl.CostEstimate(flops=2**31, bytes_accessed=2**23, transcendentals=0),
        name="prepare",
    )(parts, rows, *(array for step in steps for array in step))


def refine_kernel(start, top, *refs):
    track, pairs, (weights, offsets) = refs[0], refs[1:-2], refs[-2:]
    aheads = [track[part, : B + R] for part in range(PARTS)]
    behinds = [track[part, B + R :] for part in range(PARTS)]
    for i in range(len(pairs) // 2):
        first, second = ordered(start + i, pairs[2 * i][...], pairs[2 * i + 1][...])
        advanced(start + i, first, second, aheads, behinds)
    left = is_left(top)
    for part in range(PARTS):
        ahead, behind = aheads[part], behinds[part]
        weights[part, 0] = right_side(jnp.where(left, behind[:B], behind[B : 2 * B]))
        weights[part, 1] = right_side(jnp.where(left, 0.0, ahead[:B]))
        offsets[part, 0] = behind[2 * B :]
        offsets[part, 1] = ahead[B:]


def refine(start, top, tracked, steps):
    return pl.pallas_call(
        lambda *refs: refine_kernel(start, top, *refs),
        out_shape=(
            jax.ShapeDtypeStruct((PARTS, 2, 2 * B, 2 * B), jnp.bfloat16),
            jax.ShapeDtypeStruct((PARTS, 2, R, B), jnp.float32),
        ),
        in_specs=[pl.BlockSpec(memory_space=pltpu.VMEM)] * (1 + 2 * len(steps)),
        out_specs=[pl.BlockSpec(memory_space=pltpu.VMEM)] * 2,
        compiler_params=pltpu.CompilerParams(vmem_limit_bytes=LIMIT),
        cost_estimate=pl.CostEstimate(flops=2**30, bytes_accessed=2**22, transcendentals=0),
        name="refine",
    )(tracked, *(array for step in steps for array in step))


def finish_kernel(level, own, here, twin, weights, offsets, spread, rows, out_hbm, out, sems):
    got = jnp.concatenate(by_core(here[...], twin[...]), axis=0)
    carry = jnp.where(is_left(level), mm(own[B : B + R], got[:B]), 0.0) + got[B:]
    carry = left_side(carry)
    count = rows.shape[1]
    copies = []
    for part in range(PARTS):
        both = jnp.concatenate(
            [times(carry, weights[part, i]) + offsets[part, i] for i in range(2)], axis=1
        )
        both = jnp.concatenate(halves(both), axis=0)
        for i in range(count):
            wide = jnp.dot(both, spread[part, i], preferred_element_type=jnp.float32)
            wide = wide[:R] + wide[R:]
            out[part * count + i] = rows[part, i, 2 * B :] + wide[:, :B] + wide[:, B:]
            done = part * count + i + 1
            if done % OUT_ROWS == 0:
                span = pl.ds(done - OUT_ROWS, OUT_ROWS)
                copies.append(
                    pltpu.make_async_copy(out.at[span], out_hbm.at[span], sems.at[len(copies)])
                )
                copies[-1].start()
    for copy in copies:
        copy.wait()


def finish(level, own, here, twin, weights, offsets, spread, rows):
    shape = (rows.shape[0] * rows.shape[1], R, B)
    return pl.pallas_call(
        lambda *refs: finish_kernel(level, *refs),
        out_shape=jax.ShapeDtypeStruct(shape, jnp.float32),
        in_specs=[pl.BlockSpec(memory_space=pltpu.VMEM)] * 7,
        out_specs=pl.BlockSpec(memory_space=pltpu.HBM),
        scratch_shapes=[
            pltpu.VMEM(shape, jnp.float32),
            pltpu.SemaphoreType.DMA((shape[0] // OUT_ROWS,)),
        ],
        compiler_params=pltpu.CompilerParams(vmem_limit_bytes=LIMIT),
        name="finish",
    )(own, here, twin, weights, offsets, spread, rows)


def on_device(rhs, pivot_inv, lower_gain, upper_gain):
    devices = lax.axis_size(AXES)
    top = devices.bit_length() - 2
    plane = devices >> 3
    swap = lambda array, even, odd: lax.ppermute(
        array, AXES, [(i, i ^ (odd if i & 1 else even)) for i in range(devices)]
    )
    pack, parts, rows = local(rhs, pivot_inv, lower_gain, upper_gain)
    other = swap(pack, 1, 1)
    steps = [(pack, other)]
    pack, half = combine(pair_kernel, "pair", pack, (other,), 0, PACK // 2)
    for level, plan in PLANS:
        last = level == top - 2
        third = 6 - sum(plan)
        halves = swap(half, third << level, third << level)
        whole = swap(pack, plan[0] << level, plan[1] << level)
        if last:
            aside = prepare(parts, rows, steps)
            whole, aside = lax.optimization_barrier((whole, aside))
        received = (whole, swap(whole, 1, 1), halves, swap(halves, 1, 1))
        own = pack
        one, near, far, pack, half = combine(
            lambda *refs, level=level, plan=plan, last=last: quad_kernel(level, plan, last, *refs),
            f"quad{level}",
            own,
            received,
            3,
            (B + R) // 2 if last else PACK // 2,
        )
        steps += [(own, one), (near, far)]
    facing = [(i, FACING[i // plane] * plane + i % plane) for i in range(devices)]
    got = lax.ppermute(half, AXES, facing)
    tracked, spread = aside
    maps = refine(top - 2, top, tracked, steps[top - 2 :])
    got, maps = lax.optimization_barrier((got, maps))
    return finish(top, pack, got, swap(got, 1, 1), *maps, spread, rows)


def solution(mesh):
    placed = P(AXES, None, None)
    return jax.shard_map(
        on_device,
        mesh=mesh,
        in_specs=(placed,) * 4,
        out_specs=placed,
        check_vma=False,
    )
```

```python
import jax
import jax.numpy as jnp
from jax import lax
from jax.experimental import pallas as pl
from jax.experimental.pallas import tpu as pltpu
from jax.sharding import PartitionSpec as P

AXES = ("wide", "narrow")
B = 128
R = 64
PACK = 3 * B + 2 * R
PARTS = 2
OUT_ROWS = 3
FACING = (6, 7, 4, 5, 2, 3, 0, 1)
ROUNDS = ((1, (8, 24, 32)), (3, (2, 6, 32)), (5, (2, 6, 8)))
ASIDE_TOP = 8
LIMIT = 12 * 2**20


def halves(value):
    high = value.astype(jnp.bfloat16)
    low = (value - high.astype(jnp.float32)).astype(jnp.bfloat16)
    return high, low


def left_side(value):
    return jnp.concatenate(halves(value), axis=1)


def right_side(value):
    both = jnp.concatenate(halves(value), axis=1)
    return jnp.concatenate([both, both], axis=0)


def times(left, right):
    wide = jnp.dot(left, right, preferred_element_type=jnp.float32)
    return wide[:, :B] + wide[:, B:]


def mm(left, right):
    return times(left_side(left), right_side(right))


def local_kernel(
    rhs_hbm,
    pivot_hbm,
    lower_hbm,
    upper_hbm,
    pack,
    parts,
    rows,
    rhs,
    pivot_inv,
    lower,
    upper,
    forward,
    sems,
):
    count = rhs.shape[1]
    pairs = ((pivot_hbm, pivot_inv), (rhs_hbm, rhs), (lower_hbm, lower), (upper_hbm, upper))
    edges = (0, count // 3, count)
    spans = list(zip(edges[:-1], edges[1:]))
    waits = {}

    def fetch(which, slot, start, stop, row):
        source, target = pairs[which]
        span = (slice(None), pl.ds(start, stop - start))
        copy = pltpu.make_async_copy(source.at[span], target.at[span], sems.at[which, slot])
        copy.start()
        waits.setdefault((which // 3, row), []).append(copy)

    for slot, (start, stop) in enumerate(spans):
        for which in range(3):
            fetch(which, slot, start, stop, start)
    fetch(3, 0, 0, count, count - 1)
    states = [None] * PARTS
    scaled = {}
    for i in range(count):
        if (0, i) in waits:
            for copy in waits[0, i]:
                copy.wait()
            stop = next(stop for start, stop in spans if start == i)
            for j in range(i, stop):
                for part in range(PARTS):
                    scaled[part, j] = mm(rhs[part, j], pivot_inv[part, j])
        for part in range(PARTS):
            if i == 0:
                state = jnp.concatenate([-lower[part, 0], scaled[part, 0]], axis=0)
            else:
                moved = mm(states[part], lower[part, i])
                state = jnp.concatenate([-moved[:B], scaled[part, i] - moved[B:]], axis=0)
            forward[part, i] = state
            states[part] = state
    for part in range(PARTS):
        parts[part, : B + R] = states[part]
    for i in range(count - 1, -1, -1):
        for copy in waits.get((1, i), []):
            copy.wait()
        for part in range(PARTS):
            if i == count - 1:
                state = jnp.concatenate([-upper[part, i], states[part]], axis=0)
            else:
                moved = mm(states[part], upper[part, i])
                state = jnp.concatenate([-moved[:B], forward[part, i] - moved[B:]], axis=0)
            rows[part, i] = state
            states[part] = state
    for part in range(PARTS):
        parts[part, B + R :] = states[part]
    pack[...] = joined(parts[0], parts[1])


def local(rhs, pivot_inv, lower, upper):
    inputs = [
        pltpu.with_memory_space_constraint(
            x.reshape((PARTS, x.shape[0] // PARTS) + x.shape[1:]), pltpu.HBM
        )
        for x in (rhs, pivot_inv, lower, upper)
    ]
    count = inputs[0].shape[1]
    return pl.pallas_call(
        local_kernel,
        out_shape=(
            jax.ShapeDtypeStruct((PACK, B), jnp.float32),
            jax.ShapeDtypeStruct((PARTS, PACK, B), jnp.float32),
            jax.ShapeDtypeStruct((PARTS, count, 2 * B + R, B), jnp.float32),
        ),
        in_specs=[pl.BlockSpec(memory_space=pltpu.HBM)] * 4,
        out_specs=[pl.BlockSpec(memory_space=pltpu.VMEM)] * 3,
        scratch_shapes=[pltpu.VMEM(x.shape, jnp.float32) for x in inputs]
        + [
            pltpu.VMEM((PARTS, count, B + R, B), jnp.float32),
            pltpu.SemaphoreType.DMA((4, 2)),
        ],
        compiler_params=pltpu.CompilerParams(vmem_limit_bytes=LIMIT),
        name="local",
    )(*inputs)


def position():
    return lax.axis_index(AXES[0]) * lax.axis_size(AXES[1]) + lax.axis_index(AXES[1])


def is_left(level):
    return (position() >> level) & 1 == 0


def ordered(level, own, other):
    left = is_left(level)
    return jnp.where(left, own, other), jnp.where(left, other, own)


def turned(first, second):
    early = left_side(first[: B + R])
    turn = times(early, right_side(second[2 * B + R : 3 * B + R]))
    back = jnp.concatenate(
        [second[B + R : 2 * B + R], turn[:B], turn[B:] + second[3 * B + R :]], axis=0
    )
    return early, back


def joined(first, second):
    early, back = turned(first, second)
    down = times(early, right_side(second[:B]))
    up = mm(back, first[B + R : 2 * B + R])
    return jnp.concatenate(
        [down[:B], down[B:] + second[B : B + R], up[:B], up[B:] + first[2 * B + R :]], axis=0
    )


def pair_kernel(own, other, pack):
    pack[...] = joined(*ordered(0, own[...], other[...]))


def quad_kernel(level, own, one, two, three, near, far, pack, *send):
    mine = joined(*ordered(level, own[...], one[...]))
    theirs = joined(*ordered(level, two[...], three[...]))
    near[...] = mine
    far[...] = theirs
    value = joined(*ordered(level + 1, mine, theirs))
    pack[...] = value
    if send:
        send[0][...] = jnp.where(is_left(level + 2), value[: B + R], value[2 * B + R :])


def combine(kernel, name, own, parts, *out_rows):
    return pl.pallas_call(
        kernel,
        out_shape=tuple(jax.ShapeDtypeStruct((rows, B), jnp.float32) for rows in out_rows),
        in_specs=[pl.BlockSpec(memory_space=pltpu.VMEM)] * (1 + len(parts)),
        out_specs=[pl.BlockSpec(memory_space=pltpu.VMEM)] * len(out_rows),
        compiler_params=pltpu.CompilerParams(vmem_limit_bytes=LIMIT),
        name=name,
    )(own, *parts)


def advanced(level, first, second, ahead, behind):
    early, back = turned(first, second)
    left = is_left(level)
    through = mm(back, behind[:B])
    through = jnp.concatenate([through[:B], through[B:] + behind[B:]], axis=0)
    onward = times(early, right_side(ahead[:B]))
    onward = jnp.concatenate([onward[:B], onward[B:] + ahead[B:]], axis=0)
    cross = times(early, right_side(behind[B : 2 * B]))
    cross = jnp.concatenate([behind[:B], cross[:B], cross[B:] + behind[2 * B :]], axis=0)
    return jnp.where(left, ahead, onward), jnp.where(left, through, cross)


def identity():
    rows = lax.broadcasted_iota(jnp.int32, (2 * B + R, B), 0)
    unit = (rows == lax.broadcasted_iota(jnp.int32, (2 * B + R, B), 1)).astype(jnp.float32)
    return unit[: B + R], unit


def prepare_kernel(parts, rows, own, other, weights, offsets, spread):
    ahead, behind = identity()
    _, back = turned(parts[0], parts[1])
    maps = ((ahead, back), (parts[0, : B + R], behind))
    first, second = ordered(0, own[...], other[...])
    for part in range(PARTS):
        ahead, behind = advanced(0, first, second, *maps[part])
        weights[part, 0] = left_side(behind[: 2 * B])
        weights[part, 1] = right_side(ahead[:B])
        offsets[part, 0] = behind[2 * B :]
        offsets[part, 1] = ahead[B:]
        for i in range(rows.shape[1]):
            spread[part, i] = left_side(rows[part, i, : 2 * B])


def prepare(parts, rows, own, other):
    return pl.pallas_call(
        prepare_kernel,
        out_shape=(
            jax.ShapeDtypeStruct((PARTS, 2, 2 * B, 2 * B), jnp.bfloat16),
            jax.ShapeDtypeStruct((PARTS, 2, R, B), jnp.float32),
            jax.ShapeDtypeStruct(rows.shape[:2] + (2 * B, 2 * B), jnp.bfloat16),
        ),
        in_specs=[pl.BlockSpec(memory_space=pltpu.VMEM)] * 4,
        out_specs=[pl.BlockSpec(memory_space=pltpu.VMEM)] * 3,
        compiler_params=pltpu.CompilerParams(vmem_limit_bytes=LIMIT),
        cost_estimate=pl.CostEstimate(flops=2**31, bytes_accessed=2**23, transcendentals=0),
        name="prepare",
    )(parts, rows, own, other)


def climb_kernel(start, top, *refs):
    pairs, (weights, offsets) = refs[:-2], refs[-2:]
    ahead, behind = identity()
    for i in range(len(pairs) // 2):
        first, second = ordered(start + i, pairs[2 * i][...], pairs[2 * i + 1][...])
        ahead, behind = advanced(start + i, first, second, ahead, behind)
    left = is_left(top)
    weights[0] = right_side(jnp.where(left, behind[:B], behind[B : 2 * B]))
    weights[1] = right_side(jnp.where(left, 0.0, ahead[:B]))
    offsets[0] = behind[2 * B :]
    offsets[1] = ahead[B:]


def climb(start, top, steps):
    return pl.pallas_call(
        lambda *refs: climb_kernel(start, top, *refs),
        out_shape=(
            jax.ShapeDtypeStruct((2, 2 * B, 2 * B), jnp.bfloat16),
            jax.ShapeDtypeStruct((2, R, B), jnp.float32),
        ),
        in_specs=[pl.BlockSpec(memory_space=pltpu.VMEM)] * (2 * len(steps)),
        out_specs=[pl.BlockSpec(memory_space=pltpu.VMEM)] * 2,
        compiler_params=pltpu.CompilerParams(vmem_limit_bytes=LIMIT),
        cost_estimate=pl.CostEstimate(flops=2**31, bytes_accessed=2**23, transcendentals=0),
        name="climb",
    )(*(array for step in steps for array in step))


def carry_kernel(level, own, got, weights, offsets, carries):
    carry = jnp.where(is_left(level), mm(own[B : B + R], got[:B]), 0.0) + got[B:]
    carry = left_side(carry)
    for i in range(2):
        carries[i * R : (i + 1) * R] = times(carry, weights[i]) + offsets[i]


def carry(level, own, got, weights, offsets):
    return pl.pallas_call(
        lambda *refs: carry_kernel(level, *refs),
        out_shape=jax.ShapeDtypeStruct((2 * R, B), jnp.float32),
        in_specs=[pl.BlockSpec(memory_space=pltpu.VMEM)] * 4,
        out_specs=pl.BlockSpec(memory_space=pltpu.VMEM),
        compiler_params=pltpu.CompilerParams(vmem_limit_bytes=LIMIT),
        name="carry",
    )(own, got, weights, offsets)


def finish_kernel(here, twin, weights, offsets, spread, rows, out_hbm, out, sems):
    carries = jnp.where(position() & 1 == 0, here[...], twin[...])
    both = jnp.concatenate([carries[:R], carries[R:]], axis=1)
    both = jnp.concatenate(halves(both), axis=0)
    f_in = left_side(carries[R:])
    count = rows.shape[1]
    copies = []

    def applied(lhs, weight):
        wide = jnp.dot(lhs, weight, preferred_element_type=jnp.float32)
        wide = wide[:R] + wide[R:]
        return wide[:, :B] + wide[:, B:]

    for part in range(PARTS):
        inner = jnp.concatenate(
            [
                applied(both, weights[part, 0]) + offsets[part, 0],
                times(f_in, weights[part, 1]) + offsets[part, 1],
            ],
            axis=1,
        )
        inner = jnp.concatenate(halves(inner), axis=0)
        for i in range(count):
            out[part * count + i] = rows[part, i, 2 * B :] + applied(inner, spread[part, i])
            done = part * count + i + 1
            if done % OUT_ROWS == 0:
                span = pl.ds(done - OUT_ROWS, OUT_ROWS)
                copies.append(
                    pltpu.make_async_copy(out.at[span], out_hbm.at[span], sems.at[len(copies)])
                )
                copies[-1].start()
    for copy in copies:
        copy.wait()


def finish(here, twin, weights, offsets, spread, rows):
    shape = (rows.shape[0] * rows.shape[1], R, B)
    return pl.pallas_call(
        finish_kernel,
        out_shape=jax.ShapeDtypeStruct(shape, jnp.float32),
        in_specs=[pl.BlockSpec(memory_space=pltpu.VMEM)] * 6,
        out_specs=pl.BlockSpec(memory_space=pltpu.HBM),
        scratch_shapes=[
            pltpu.VMEM(shape, jnp.float32),
            pltpu.SemaphoreType.DMA((shape[0] // OUT_ROWS,)),
        ],
        compiler_params=pltpu.CompilerParams(vmem_limit_bytes=LIMIT),
        name="finish",
    )(here, twin, weights, offsets, spread, rows)


def on_device(rhs, pivot_inv, lower_gain, upper_gain):
    devices = lax.axis_size(AXES)
    top = devices.bit_length() - 2
    plane = devices >> 3

    def swap(array, even, odd):
        pairs = [(i, i ^ (odd if i & 1 else even)) for i in range(devices)]
        return lax.ppermute(array, AXES, pairs)

    own, parts, rows = local(rhs, pivot_inv, lower_gain, upper_gain)
    other = swap(own, 1, 1)
    (pack,) = combine(pair_kernel, "pair", own, (other,), PACK)
    steps = []
    for level, aside in ROUNDS:
        last = level == top - 2
        gots = tuple(swap(pack, bits << level, aside[bits - 1]) for bits in (1, 2, 3))
        if level == 1:
            maps = prepare(parts, rows, own, other)
            gots, maps = lax.optimization_barrier((gots, maps))
        near, far, joint, *send = combine(
            lambda *refs, level=level: quad_kernel(level, *refs),
            f"quad{level}",
            pack,
            gots,
            *(PACK,) * 3,
            *((B + R,) if last else ()),
        )
        steps += [(pack, gots[0]), (near, far)]
        pack = joint
    facing = [
        (i, i ^ ASIDE_TOP if i & 1 else FACING[i // plane] * plane + i % plane)
        for i in range(devices)
    ]
    got = lax.ppermute(send[0], AXES, facing)
    climbed = climb(1, top, steps)
    got, climbed = lax.optimization_barrier((got, climbed))
    here = carry(top, pack, got, *climbed)
    return finish(here, swap(here, 1, 1), *maps, rows)


def solution(mesh):
    placed = P(AXES, None, None)
    return jax.shard_map(
        on_device,
        mesh=mesh,
        in_specs=(placed,) * 4,
        out_specs=placed,
        check_vma=False,
    )
```

```python
import jax
import jax.numpy as jnp
from jax import lax
from jax.experimental import pallas as pl
from jax.experimental.pallas import tpu as pltpu
from jax.sharding import PartitionSpec as P

AXES = ("wide", "narrow")
B = 128
R = 64
PACK = 3 * B + 2 * R
PARTS = 2
OUT_ROWS = 3
FACING = (7, 6, 5, 4, 3, 2, 1, 0)
PLANS = ((1, (1, 2)), (3, (1, 2)), (5, (1, 3)))
LIMIT = 12 * 2**20


def halves(value):
    high = value.astype(jnp.bfloat16)
    low = (value - high.astype(jnp.float32)).astype(jnp.bfloat16)
    return high, low


def left_side(value):
    return jnp.concatenate(halves(value), axis=1)


def right_side(value):
    both = jnp.concatenate(halves(value), axis=1)
    return jnp.concatenate([both, both], axis=0)


def times(left, right):
    wide = jnp.dot(left, right, preferred_element_type=jnp.float32)
    return wide[:, :B] + wide[:, B:]


def mm(left, right):
    return times(left_side(left), right_side(right))


def local_kernel(
    rhs_hbm,
    pivot_hbm,
    lower_hbm,
    upper_hbm,
    pack,
    parts,
    rows,
    rhs,
    pivot_inv,
    lower,
    upper,
    forward,
    sems,
):
    count = rhs.shape[1]
    pairs = ((pivot_hbm, pivot_inv), (rhs_hbm, rhs), (lower_hbm, lower), (upper_hbm, upper))
    edges = (0, count // 3, count)
    spans = list(zip(edges[:-1], edges[1:]))
    waits = {}

    def fetch(which, slot, start, stop, row):
        source, target = pairs[which]
        span = (slice(None), pl.ds(start, stop - start))
        copy = pltpu.make_async_copy(source.at[span], target.at[span], sems.at[which, slot])
        copy.start()
        waits.setdefault((which // 3, row), []).append(copy)

    for slot, (start, stop) in enumerate(spans):
        for which in range(3):
            fetch(which, slot, start, stop, start)
    fetch(3, 0, 0, count, count - 1)
    states = [None] * PARTS
    scaled = {}
    for i in range(count):
        if (0, i) in waits:
            for copy in waits[0, i]:
                copy.wait()
            stop = next(stop for start, stop in spans if start == i)
            for j in range(i, stop):
                for part in range(PARTS):
                    scaled[part, j] = mm(rhs[part, j], pivot_inv[part, j])
        for part in range(PARTS):
            if i == 0:
                state = jnp.concatenate([-lower[part, 0], scaled[part, 0]], axis=0)
            else:
                moved = mm(states[part], lower[part, i])
                state = jnp.concatenate([-moved[:B], scaled[part, i] - moved[B:]], axis=0)
            forward[part, i] = state
            states[part] = state
    for part in range(PARTS):
        parts[part, : B + R] = states[part]
    for i in range(count - 1, -1, -1):
        for copy in waits.get((1, i), []):
            copy.wait()
        for part in range(PARTS):
            if i == count - 1:
                state = jnp.concatenate([-upper[part, i], states[part]], axis=0)
            else:
                moved = mm(states[part], upper[part, i])
                state = jnp.concatenate([-moved[:B], forward[part, i] - moved[B:]], axis=0)
            rows[part, i] = state
            states[part] = state
    for part in range(PARTS):
        parts[part, B + R :] = states[part]
    pack[...] = joined(parts[0], parts[1])


def local(rhs, pivot_inv, lower, upper):
    inputs = [
        pltpu.with_memory_space_constraint(
            x.reshape((PARTS, x.shape[0] // PARTS) + x.shape[1:]), pltpu.HBM
        )
        for x in (rhs, pivot_inv, lower, upper)
    ]
    count = inputs[0].shape[1]
    return pl.pallas_call(
        local_kernel,
        out_shape=(
            jax.ShapeDtypeStruct((PACK, B), jnp.float32),
            jax.ShapeDtypeStruct((PARTS, PACK, B), jnp.float32),
            jax.ShapeDtypeStruct((PARTS, count, 2 * B + R, B), jnp.float32),
        ),
        in_specs=[pl.BlockSpec(memory_space=pltpu.HBM)] * 4,
        out_specs=[pl.BlockSpec(memory_space=pltpu.VMEM)] * 3,
        scratch_shapes=[pltpu.VMEM(x.shape, jnp.float32) for x in inputs]
        + [
            pltpu.VMEM((PARTS, count, B + R, B), jnp.float32),
            pltpu.SemaphoreType.DMA((4, 2)),
        ],
        compiler_params=pltpu.CompilerParams(vmem_limit_bytes=LIMIT),
        name="local",
    )(*inputs)


def position():
    return lax.axis_index(AXES[0]) * lax.axis_size(AXES[1]) + lax.axis_index(AXES[1])


def is_left(level):
    return (position() >> level) & 1 == 0


def ordered(level, own, other):
    left = is_left(level)
    return jnp.where(left, own, other), jnp.where(left, other, own)


def by_core(here, there):
    low = position() & 1 == 0
    return jnp.where(low, here, there), jnp.where(low, there, here)


def turned(first, second):
    early = left_side(first[: B + R])
    turn = times(early, right_side(second[2 * B + R : 3 * B + R]))
    back = jnp.concatenate(
        [second[B + R : 2 * B + R], turn[:B], turn[B:] + second[3 * B + R :]], axis=0
    )
    return early, back


def joined(first, second):
    early, back = turned(first, second)
    down = times(early, right_side(second[:B]))
    up = mm(back, first[B + R : 2 * B + R])
    return jnp.concatenate(
        [down[:B], down[B:] + second[B : B + R], up[:B], up[B:] + first[2 * B + R :]], axis=0
    )


def store_half(send, pack):
    half = pack.shape[0] // 2
    send[...] = jnp.where(position() & 1 == 0, pack[:half], pack[half:])


def pair_kernel(own, other, pack, send):
    value = joined(*ordered(0, own[...], other[...]))
    pack[...] = value
    store_half(send, value)


def quad_kernel(level, plan, top, *refs):
    own, whole, whole_twin, half, half_twin, one, near, far, pack, send = refs
    partner = dict(zip(plan, by_core(whole[...], whole_twin[...])))
    partner[6 - sum(plan)] = jnp.concatenate(by_core(half[...], half_twin[...]), axis=0)
    one[...] = partner[1]
    mine = joined(*ordered(level, own[...], partner[1]))
    theirs = joined(*ordered(level, partner[2], partner[3]))
    near[...] = mine
    far[...] = theirs
    value = joined(*ordered(level + 1, mine, theirs))
    pack[...] = value
    if top:
        store_half(send, jnp.where(is_left(level + 2), value[: B + R], value[2 * B + R :]))
    else:
        store_half(send, value)


def combine(kernel, name, own, parts, extra, send_rows):
    whole = jax.ShapeDtypeStruct((PACK, B), jnp.float32)
    return pl.pallas_call(
        kernel,
        out_shape=(whole,) * (1 + extra) + (jax.ShapeDtypeStruct((send_rows, B), jnp.float32),),
        in_specs=[pl.BlockSpec(memory_space=pltpu.VMEM)] * (1 + len(parts)),
        out_specs=[pl.BlockSpec(memory_space=pltpu.VMEM)] * (2 + extra),
        compiler_params=pltpu.CompilerParams(vmem_limit_bytes=LIMIT),
        name=name,
    )(own, *parts)


def advanced(level, first, second, aheads, behinds):
    early, back = turned(first, second)
    late = left_side(back)
    left = is_left(level)
    for part in range(PARTS):
        ahead, behind = aheads[part], behinds[part]
        through = times(late, right_side(behind[:B]))
        through = jnp.concatenate([through[:B], through[B:] + behind[B:]], axis=0)
        onward = times(early, right_side(ahead[:B]))
        onward = jnp.concatenate([onward[:B], onward[B:] + ahead[B:]], axis=0)
        cross = times(early, right_side(behind[B : 2 * B]))
        cross = jnp.concatenate([behind[:B], cross[:B], cross[B:] + behind[2 * B :]], axis=0)
        aheads[part] = jnp.where(left, ahead, onward)
        behinds[part] = jnp.where(left, through, cross)


def prepare_kernel(levels, *refs):
    parts, rows, pairs, (track, spread) = refs[0], refs[1], refs[2:-2], refs[-2:]
    eye = (
        lax.broadcasted_iota(jnp.int32, (B, B), 0) == lax.broadcasted_iota(jnp.int32, (B, B), 1)
    ).astype(jnp.float32)
    none = jnp.zeros((B + R, B), jnp.float32)
    _, back = turned(parts[0], parts[1])
    aheads = [jnp.concatenate([eye, none[:R]], axis=0), parts[0, : B + R]]
    behinds = [back, jnp.concatenate([eye, none], axis=0)]
    for level in range(levels):
        first, second = ordered(level, pairs[2 * level][...], pairs[2 * level + 1][...])
        advanced(level, first, second, aheads, behinds)
    for part in range(PARTS):
        track[part, : B + R] = aheads[part]
        track[part, B + R :] = behinds[part]
        for i in range(rows.shape[1]):
            spread[part, i] = left_side(rows[part, i, : 2 * B])


def prepare(parts, rows, steps):
    return pl.pallas_call(
        lambda *refs: prepare_kernel(len(steps), *refs),
        out_shape=(
            jax.ShapeDtypeStruct((PARTS, PACK, B), jnp.float32),
            jax.ShapeDtypeStruct(rows.shape[:2] + (2 * B, 2 * B), jnp.bfloat16),
        ),
        in_specs=[pl.BlockSpec(memory_space=pltpu.VMEM)] * (2 + 2 * len(steps)),
        out_specs=[pl.BlockSpec(memory_space=pltpu.VMEM)] * 2,
        compiler_params=pltpu.CompilerParams(vmem_limit_bytes=LIMIT),
        cost_estimate=pl.CostEstimate(flops=2**31, bytes_accessed=2**23, transcendentals=0),
        name="prepare",
    )(parts, rows, *(array for step in steps for array in step))


def refine_kernel(start, top, *refs):
    track, pairs, (weights, offsets) = refs[0], refs[1:-2], refs[-2:]
    aheads = [track[part, : B + R] for part in range(PARTS)]
    behinds = [track[part, B + R :] for part in range(PARTS)]
    for i in range(len(pairs) // 2):
        first, second = ordered(start + i, pairs[2 * i][...], pairs[2 * i + 1][...])
        advanced(start + i, first, second, aheads, behinds)
    left = is_left(top)
    for part in range(PARTS):
        ahead, behind = aheads[part], behinds[part]
        weights[part, 0] = right_side(jnp.where(left, behind[:B], behind[B : 2 * B]))
        weights[part, 1] = right_side(jnp.where(left, 0.0, ahead[:B]))
        offsets[part, 0] = behind[2 * B :]
        offsets[part, 1] = ahead[B:]


def refine(start, top, tracked, steps):
    return pl.pallas_call(
        lambda *refs: refine_kernel(start, top, *refs),
        out_shape=(
            jax.ShapeDtypeStruct((PARTS, 2, 2 * B, 2 * B), jnp.bfloat16),
            jax.ShapeDtypeStruct((PARTS, 2, R, B), jnp.float32),
        ),
        in_specs=[pl.BlockSpec(memory_space=pltpu.VMEM)] * (1 + 2 * len(steps)),
        out_specs=[pl.BlockSpec(memory_space=pltpu.VMEM)] * 2,
        compiler_params=pltpu.CompilerParams(vmem_limit_bytes=LIMIT),
        cost_estimate=pl.CostEstimate(flops=2**30, bytes_accessed=2**22, transcendentals=0),
        name="refine",
    )(tracked, *(array for step in steps for array in step))


def finish_kernel(level, own, here, twin, weights, offsets, spread, rows, out_hbm, out, sems):
    got = jnp.concatenate(by_core(here[...], twin[...]), axis=0)
    carry = jnp.where(is_left(level), mm(own[B : B + R], got[:B]), 0.0) + got[B:]
    carry = left_side(carry)
    count = rows.shape[1]
    copies = []
    for part in range(PARTS):
        both = jnp.concatenate(
            [times(carry, weights[part, i]) + offsets[part, i] for i in range(2)], axis=1
        )
        both = jnp.concatenate(halves(both), axis=0)
        for i in range(count):
            wide = jnp.dot(both, spread[part, i], preferred_element_type=jnp.float32)
            wide = wide[:R] + wide[R:]
            out[part * count + i] = rows[part, i, 2 * B :] + wide[:, :B] + wide[:, B:]
            done = part * count + i + 1
            if done % OUT_ROWS == 0:
                span = pl.ds(done - OUT_ROWS, OUT_ROWS)
                copies.append(
                    pltpu.make_async_copy(out.at[span], out_hbm.at[span], sems.at[len(copies)])
                )
                copies[-1].start()
    for copy in copies:
        copy.wait()


def finish(level, own, here, twin, weights, offsets, spread, rows):
    shape = (rows.shape[0] * rows.shape[1], R, B)
    return pl.pallas_call(
        lambda *refs: finish_kernel(level, *refs),
        out_shape=jax.ShapeDtypeStruct(shape, jnp.float32),
        in_specs=[pl.BlockSpec(memory_space=pltpu.VMEM)] * 7,
        out_specs=pl.BlockSpec(memory_space=pltpu.HBM),
        scratch_shapes=[
            pltpu.VMEM(shape, jnp.float32),
            pltpu.SemaphoreType.DMA((shape[0] // OUT_ROWS,)),
        ],
        compiler_params=pltpu.CompilerParams(vmem_limit_bytes=LIMIT),
        name="finish",
    )(own, here, twin, weights, offsets, spread, rows)


def on_device(rhs, pivot_inv, lower_gain, upper_gain):
    devices = lax.axis_size(AXES)
    top = devices.bit_length() - 2
    plane = devices >> 3
    swap = lambda array, even, odd: lax.ppermute(
        array, AXES, [(i, i ^ (odd if i & 1 else even)) for i in range(devices)]
    )
    pack, parts, rows = local(rhs, pivot_inv, lower_gain, upper_gain)
    other = swap(pack, 1, 1)
    steps = [(pack, other)]
    pack, half = combine(pair_kernel, "pair", pack, (other,), 0, PACK // 2)
    for level, plan in PLANS:
        last = level == top - 2
        third = 6 - sum(plan)
        halves = swap(half, third << level, third << level)
        whole = swap(pack, plan[0] << level, plan[1] << level)
        if last:
            aside = prepare(parts, rows, steps)
            whole, aside = lax.optimization_barrier((whole, aside))
        received = (whole, swap(whole, 1, 1), halves, swap(halves, 1, 1))
        own = pack
        one, near, far, pack, half = combine(
            lambda *refs, level=level, plan=plan, last=last: quad_kernel(level, plan, last, *refs),
            f"quad{level}",
            own,
            received,
            3,
            (B + R) // 2 if last else PACK // 2,
        )
        steps += [(own, one), (near, far)]
    facing = [(i, FACING[i // plane] * plane + i % plane) for i in range(devices)]
    got = lax.ppermute(half, AXES, facing)
    tracked, spread = aside
    maps = refine(top - 2, top, tracked, steps[top - 2 :])
    got, maps = lax.optimization_barrier((got, maps))
    return finish(top, pack, got, swap(got, 1, 1), *maps, spread, rows)


def solution(mesh):
    placed = P(AXES, None, None)
    return jax.shard_map(
        on_device,
        mesh=mesh,
        in_specs=(placed,) * 4,
        out_specs=placed,
        check_vma=False,
    )
```

```python
import jax
import jax.numpy as jnp
from jax import lax
from jax.experimental import pallas as pl
from jax.experimental.pallas import tpu as pltpu
from jax.sharding import PartitionSpec as P

AXES = ("wide", "narrow")
B = 128
R = 64
PACK = 3 * B + 2 * R
PARTS = 2
OUT_ROWS = 3
FACING = (6, 5, 4, 7, 2, 1, 0, 3)
PLANS = ((1, (1, 2)), (3, (1, 2)), (5, (1, 3)))
LIMIT = 12 * 2**20


def halves(value):
    high = value.astype(jnp.bfloat16)
    low = (value - high.astype(jnp.float32)).astype(jnp.bfloat16)
    return high, low


def left_side(value):
    return jnp.concatenate(halves(value), axis=1)


def right_side(value):
    both = jnp.concatenate(halves(value), axis=1)
    return jnp.concatenate([both, both], axis=0)


def times(left, right):
    wide = jnp.dot(left, right, preferred_element_type=jnp.float32)
    return wide[:, :B] + wide[:, B:]


def mm(left, right):
    return times(left_side(left), right_side(right))


def local_kernel(
    rhs_hbm,
    pivot_hbm,
    lower_hbm,
    upper_hbm,
    pack,
    parts,
    rows,
    rhs,
    pivot_inv,
    lower,
    upper,
    forward,
    sems,
):
    count = rhs.shape[1]
    pairs = ((pivot_hbm, pivot_inv), (rhs_hbm, rhs), (lower_hbm, lower), (upper_hbm, upper))
    edges = (0, count // 3, count)
    spans = list(zip(edges[:-1], edges[1:]))
    waits = {}

    def fetch(which, slot, start, stop, row):
        source, target = pairs[which]
        span = (slice(None), pl.ds(start, stop - start))
        copy = pltpu.make_async_copy(source.at[span], target.at[span], sems.at[which, slot])
        copy.start()
        waits.setdefault((which // 3, row), []).append(copy)

    for slot, (start, stop) in enumerate(spans):
        for which in range(3):
            fetch(which, slot, start, stop, start)
    fetch(3, 0, 0, count, count - 1)
    states = [None] * PARTS
    scaled = {}
    for i in range(count):
        if (0, i) in waits:
            for copy in waits[0, i]:
                copy.wait()
            stop = next(stop for start, stop in spans if start == i)
            for j in range(i, stop):
                for part in range(PARTS):
                    scaled[part, j] = mm(rhs[part, j], pivot_inv[part, j])
        for part in range(PARTS):
            if i == 0:
                state = jnp.concatenate([-lower[part, 0], scaled[part, 0]], axis=0)
            else:
                moved = mm(states[part], lower[part, i])
                state = jnp.concatenate([-moved[:B], scaled[part, i] - moved[B:]], axis=0)
            forward[part, i] = state
            states[part] = state
    for part in range(PARTS):
        parts[part, : B + R] = states[part]
    for i in range(count - 1, -1, -1):
        for copy in waits.get((1, i), []):
            copy.wait()
        for part in range(PARTS):
            if i == count - 1:
                state = jnp.concatenate([-upper[part, i], states[part]], axis=0)
            else:
                moved = mm(states[part], upper[part, i])
                state = jnp.concatenate([-moved[:B], forward[part, i] - moved[B:]], axis=0)
            rows[part, i] = state
            states[part] = state
    for part in range(PARTS):
        parts[part, B + R :] = states[part]
    pack[...] = joined(parts[0], parts[1])


def local(rhs, pivot_inv, lower, upper):
    inputs = [
        pltpu.with_memory_space_constraint(
            x.reshape((PARTS, x.shape[0] // PARTS) + x.shape[1:]), pltpu.HBM
        )
        for x in (rhs, pivot_inv, lower, upper)
    ]
    count = inputs[0].shape[1]
    return pl.pallas_call(
        local_kernel,
        out_shape=(
            jax.ShapeDtypeStruct((PACK, B), jnp.float32),
            jax.ShapeDtypeStruct((PARTS, PACK, B), jnp.float32),
            jax.ShapeDtypeStruct((PARTS, count, 2 * B + R, B), jnp.float32),
        ),
        in_specs=[pl.BlockSpec(memory_space=pltpu.HBM)] * 4,
        out_specs=[pl.BlockSpec(memory_space=pltpu.VMEM)] * 3,
        scratch_shapes=[pltpu.VMEM(x.shape, jnp.float32) for x in inputs]
        + [
            pltpu.VMEM((PARTS, count, B + R, B), jnp.float32),
            pltpu.SemaphoreType.DMA((4, 2)),
        ],
        compiler_params=pltpu.CompilerParams(vmem_limit_bytes=LIMIT),
        name="local",
    )(*inputs)


def position():
    return lax.axis_index(AXES[0]) * lax.axis_size(AXES[1]) + lax.axis_index(AXES[1])


def is_left(level):
    return (position() >> level) & 1 == 0


def ordered(level, own, other):
    left = is_left(level)
    return jnp.where(left, own, other), jnp.where(left, other, own)


def by_core(here, there):
    low = position() & 1 == 0
    return jnp.where(low, here, there), jnp.where(low, there, here)


def turned(first, second):
    early = left_side(first[: B + R])
    turn = times(early, right_side(second[2 * B + R : 3 * B + R]))
    back = jnp.concatenate(
        [second[B + R : 2 * B + R], turn[:B], turn[B:] + second[3 * B + R :]], axis=0
    )
    return early, back


def joined(first, second):
    early, back = turned(first, second)
    down = times(early, right_side(second[:B]))
    up = mm(back, first[B + R : 2 * B + R])
    return jnp.concatenate(
        [down[:B], down[B:] + second[B : B + R], up[:B], up[B:] + first[2 * B + R :]], axis=0
    )


def store_half(send, pack):
    half = pack.shape[0] // 2
    send[...] = jnp.where(position() & 1 == 0, pack[:half], pack[half:])


def pair_kernel(own, other, pack, send):
    value = joined(*ordered(0, own[...], other[...]))
    pack[...] = value
    store_half(send, value)


def quad_kernel(level, plan, top, *refs):
    own, whole, whole_twin, half, half_twin, one, near, far, pack, send = refs
    partner = dict(zip(plan, by_core(whole[...], whole_twin[...])))
    partner[6 - sum(plan)] = jnp.concatenate(by_core(half[...], half_twin[...]), axis=0)
    one[...] = partner[1]
    mine = joined(*ordered(level, own[...], partner[1]))
    theirs = joined(*ordered(level, partner[2], partner[3]))
    near[...] = mine
    far[...] = theirs
    value = joined(*ordered(level + 1, mine, theirs))
    pack[...] = value
    if top:
        store_half(send, jnp.where(is_left(level + 2), value[: B + R], value[2 * B + R :]))
    else:
        store_half(send, value)


def combine(kernel, name, own, parts, extra, send_rows):
    whole = jax.ShapeDtypeStruct((PACK, B), jnp.float32)
    return pl.pallas_call(
        kernel,
        out_shape=(whole,) * (1 + extra) + (jax.ShapeDtypeStruct((send_rows, B), jnp.float32),),
        in_specs=[pl.BlockSpec(memory_space=pltpu.VMEM)] * (1 + len(parts)),
        out_specs=[pl.BlockSpec(memory_space=pltpu.VMEM)] * (2 + extra),
        compiler_params=pltpu.CompilerParams(vmem_limit_bytes=LIMIT),
        name=name,
    )(own, *parts)


def advanced(level, first, second, aheads, behinds):
    early, back = turned(first, second)
    late = left_side(back)
    left = is_left(level)
    for part in range(PARTS):
        ahead, behind = aheads[part], behinds[part]
        through = times(late, right_side(behind[:B]))
        through = jnp.concatenate([through[:B], through[B:] + behind[B:]], axis=0)
        onward = times(early, right_side(ahead[:B]))
        onward = jnp.concatenate([onward[:B], onward[B:] + ahead[B:]], axis=0)
        cross = times(early, right_side(behind[B : 2 * B]))
        cross = jnp.concatenate([behind[:B], cross[:B], cross[B:] + behind[2 * B :]], axis=0)
        aheads[part] = jnp.where(left, ahead, onward)
        behinds[part] = jnp.where(left, through, cross)


def prepare_kernel(levels, *refs):
    parts, rows, pairs, (track, spread) = refs[0], refs[1], refs[2:-2], refs[-2:]
    eye = (
        lax.broadcasted_iota(jnp.int32, (B, B), 0) == lax.broadcasted_iota(jnp.int32, (B, B), 1)
    ).astype(jnp.float32)
    none = jnp.zeros((B + R, B), jnp.float32)
    _, back = turned(parts[0], parts[1])
    aheads = [jnp.concatenate([eye, none[:R]], axis=0), parts[0, : B + R]]
    behinds = [back, jnp.concatenate([eye, none], axis=0)]
    for level in range(levels):
        first, second = ordered(level, pairs[2 * level][...], pairs[2 * level + 1][...])
        advanced(level, first, second, aheads, behinds)
    for part in range(PARTS):
        track[part, : B + R] = aheads[part]
        track[part, B + R :] = behinds[part]
        for i in range(rows.shape[1]):
            spread[part, i] = left_side(rows[part, i, : 2 * B])


def prepare(parts, rows, steps):
    return pl.pallas_call(
        lambda *refs: prepare_kernel(len(steps), *refs),
        out_shape=(
            jax.ShapeDtypeStruct((PARTS, PACK, B), jnp.float32),
            jax.ShapeDtypeStruct(rows.shape[:2] + (2 * B, 2 * B), jnp.bfloat16),
        ),
        in_specs=[pl.BlockSpec(memory_space=pltpu.VMEM)] * (2 + 2 * len(steps)),
        out_specs=[pl.BlockSpec(memory_space=pltpu.VMEM)] * 2,
        compiler_params=pltpu.CompilerParams(vmem_limit_bytes=LIMIT),
        cost_estimate=pl.CostEstimate(flops=2**31, bytes_accessed=2**23, transcendentals=0),
        name="prepare",
    )(parts, rows, *(array for step in steps for array in step))


def refine_kernel(start, top, *refs):
    track, pairs, (weights, offsets) = refs[0], refs[1:-2], refs[-2:]
    aheads = [track[part, : B + R] for part in range(PARTS)]
    behinds = [track[part, B + R :] for part in range(PARTS)]
    for i in range(len(pairs) // 2):
        first, second = ordered(start + i, pairs[2 * i][...], pairs[2 * i + 1][...])
        advanced(start + i, first, second, aheads, behinds)
    left = is_left(top)
    for part in range(PARTS):
        ahead, behind = aheads[part], behinds[part]
        weights[part, 0] = right_side(jnp.where(left, behind[:B], behind[B : 2 * B]))
        weights[part, 1] = right_side(jnp.where(left, 0.0, ahead[:B]))
        offsets[part, 0] = behind[2 * B :]
        offsets[part, 1] = ahead[B:]


def refine(start, top, tracked, steps):
    return pl.pallas_call(
        lambda *refs: refine_kernel(start, top, *refs),
        out_shape=(
            jax.ShapeDtypeStruct((PARTS, 2, 2 * B, 2 * B), jnp.bfloat16),
            jax.ShapeDtypeStruct((PARTS, 2, R, B), jnp.float32),
        ),
        in_specs=[pl.BlockSpec(memory_space=pltpu.VMEM)] * (1 + 2 * len(steps)),
        out_specs=[pl.BlockSpec(memory_space=pltpu.VMEM)] * 2,
        compiler_params=pltpu.CompilerParams(vmem_limit_bytes=LIMIT),
        cost_estimate=pl.CostEstimate(flops=2**30, bytes_accessed=2**22, transcendentals=0),
        name="refine",
    )(tracked, *(array for step in steps for array in step))


def finish_kernel(level, own, here, twin, weights, offsets, spread, rows, out_hbm, out, sems):
    got = jnp.concatenate(by_core(here[...], twin[...]), axis=0)
    carry = jnp.where(is_left(level), mm(own[B : B + R], got[:B]), 0.0) + got[B:]
    carry = left_side(carry)
    count = rows.shape[1]
    copies = []
    for part in range(PARTS):
        both = jnp.concatenate(
            [times(carry, weights[part, i]) + offsets[part, i] for i in range(2)], axis=1
        )
        both = jnp.concatenate(halves(both), axis=0)
        for i in range(count):
            wide = jnp.dot(both, spread[part, i], preferred_element_type=jnp.float32)
            wide = wide[:R] + wide[R:]
            out[part * count + i] = rows[part, i, 2 * B :] + wide[:, :B] + wide[:, B:]
            done = part * count + i + 1
            if done % OUT_ROWS == 0:
                span = pl.ds(done - OUT_ROWS, OUT_ROWS)
                copies.append(
                    pltpu.make_async_copy(out.at[span], out_hbm.at[span], sems.at[len(copies)])
                )
                copies[-1].start()
    for copy in copies:
        copy.wait()


def finish(level, own, here, twin, weights, offsets, spread, rows):
    shape = (rows.shape[0] * rows.shape[1], R, B)
    return pl.pallas_call(
        lambda *refs: finish_kernel(level, *refs),
        out_shape=jax.ShapeDtypeStruct(shape, jnp.float32),
        in_specs=[pl.BlockSpec(memory_space=pltpu.VMEM)] * 7,
        out_specs=pl.BlockSpec(memory_space=pltpu.HBM),
        scratch_shapes=[
            pltpu.VMEM(shape, jnp.float32),
            pltpu.SemaphoreType.DMA((shape[0] // OUT_ROWS,)),
        ],
        compiler_params=pltpu.CompilerParams(vmem_limit_bytes=LIMIT),
        name="finish",
    )(own, here, twin, weights, offsets, spread, rows)


def on_device(rhs, pivot_inv, lower_gain, upper_gain):
    devices = lax.axis_size(AXES)
    top = devices.bit_length() - 2
    plane = devices >> 3
    swap = lambda array, even, odd: lax.ppermute(
        array, AXES, [(i, i ^ (odd if i & 1 else even)) for i in range(devices)]
    )
    pack, parts, rows = local(rhs, pivot_inv, lower_gain, upper_gain)
    other = swap(pack, 1, 1)
    steps = [(pack, other)]
    pack, half = combine(pair_kernel, "pair", pack, (other,), 0, PACK // 2)
    for level, plan in PLANS:
        last = level == top - 2
        third = 6 - sum(plan)
        halves = swap(half, third << level, third << level)
        whole = swap(pack, plan[0] << level, plan[1] << level)
        if last:
            aside = prepare(parts, rows, steps)
            whole, aside = lax.optimization_barrier((whole, aside))
        received = (whole, swap(whole, 1, 1), halves, swap(halves, 1, 1))
        own = pack
        one, near, far, pack, half = combine(
            lambda *refs, level=level, plan=plan, last=last: quad_kernel(level, plan, last, *refs),
            f"quad{level}",
            own,
            received,
            3,
            (B + R) // 2 if last else PACK // 2,
        )
        steps += [(own, one), (near, far)]
    facing = [(i, FACING[i // plane] * plane + i % plane) for i in range(devices)]
    got = lax.ppermute(half, AXES, facing)
    tracked, spread = aside
    maps = refine(top - 2, top, tracked, steps[top - 2 :])
    got, maps = lax.optimization_barrier((got, maps))
    return finish(top, pack, got, swap(got, 1, 1), *maps, spread, rows)


def solution(mesh):
    placed = P(AXES, None, None)
    return jax.shard_map(
        on_device,
        mesh=mesh,
        in_specs=(placed,) * 4,
        out_specs=placed,
        check_vma=False,
    )
```

```python
import jax
import jax.numpy as jnp
from jax import lax
from jax.experimental import pallas as pl
from jax.experimental.pallas import tpu as pltpu
from jax.sharding import PartitionSpec as P

AXES = ("wide", "narrow")
B = 128
R = 64
PACK = 3 * B + 2 * R
PARTS = 2
OUT_ROWS = 3
FACING = (6, 7, 4, 5, 2, 3, 0, 1)
PLANS = ((1, (1, 2)), (3, (1, 2)), (5, (1, 3)))
LIMIT = 12 * 2**20


def halves(value):
    high = value.astype(jnp.bfloat16)
    low = (value - high.astype(jnp.float32)).astype(jnp.bfloat16)
    return high, low


def left_side(value):
    return jnp.concatenate(halves(value), axis=1)


def right_side(value):
    both = jnp.concatenate(halves(value), axis=1)
    return jnp.concatenate([both, both], axis=0)


def times(left, right):
    wide = jnp.dot(left, right, preferred_element_type=jnp.float32)
    return wide[:, :B] + wide[:, B:]


def mm(left, right):
    return times(left_side(left), right_side(right))


def local_kernel(
    rhs_hbm,
    pivot_hbm,
    lower_hbm,
    upper_hbm,
    pack,
    parts,
    rows,
    rhs,
    pivot_inv,
    lower,
    upper,
    forward,
    sems,
):
    count = rhs.shape[1]
    pairs = ((pivot_hbm, pivot_inv), (rhs_hbm, rhs), (lower_hbm, lower), (upper_hbm, upper))
    edges = (0, count // 3, count)
    spans = list(zip(edges[:-1], edges[1:]))
    waits = {}

    def fetch(which, slot, start, stop, row):
        source, target = pairs[which]
        span = (slice(None), pl.ds(start, stop - start))
        copy = pltpu.make_async_copy(source.at[span], target.at[span], sems.at[which, slot])
        copy.start()
        waits.setdefault((which // 3, row), []).append(copy)

    for slot, (start, stop) in enumerate(spans):
        for which in range(3):
            fetch(which, slot, start, stop, start)
    fetch(3, 0, 0, count, count - 1)
    states = [None] * PARTS
    scaled = {}
    for i in range(count):
        if (0, i) in waits:
            for copy in waits[0, i]:
                copy.wait()
            stop = next(stop for start, stop in spans if start == i)
            for j in range(i, stop):
                for part in range(PARTS):
                    scaled[part, j] = mm(rhs[part, j], pivot_inv[part, j])
        for part in range(PARTS):
            if i == 0:
                state = jnp.concatenate([-lower[part, 0], scaled[part, 0]], axis=0)
            else:
                moved = mm(states[part], lower[part, i])
                state = jnp.concatenate([-moved[:B], scaled[part, i] - moved[B:]], axis=0)
            forward[part, i] = state
            states[part] = state
    for part in range(PARTS):
        parts[part, : B + R] = states[part]
    for i in range(count - 1, -1, -1):
        for copy in waits.get((1, i), []):
            copy.wait()
        for part in range(PARTS):
            if i == count - 1:
                state = jnp.concatenate([-upper[part, i], states[part]], axis=0)
            else:
                moved = mm(states[part], upper[part, i])
                state = jnp.concatenate([-moved[:B], forward[part, i] - moved[B:]], axis=0)
            rows[part, i] = state
            states[part] = state
    for part in range(PARTS):
        parts[part, B + R :] = states[part]
    pack[...] = joined(parts[0], parts[1])


def local(rhs, pivot_inv, lower, upper):
    inputs = [
        pltpu.with_memory_space_constraint(
            x.reshape((PARTS, x.shape[0] // PARTS) + x.shape[1:]), pltpu.HBM
        )
        for x in (rhs, pivot_inv, lower, upper)
    ]
    count = inputs[0].shape[1]
    return pl.pallas_call(
        local_kernel,
        out_shape=(
            jax.ShapeDtypeStruct((PACK, B), jnp.float32),
            jax.ShapeDtypeStruct((PARTS, PACK, B), jnp.float32),
            jax.ShapeDtypeStruct((PARTS, count, 2 * B + R, B), jnp.float32),
        ),
        in_specs=[pl.BlockSpec(memory_space=pltpu.HBM)] * 4,
        out_specs=[pl.BlockSpec(memory_space=pltpu.VMEM)] * 3,
        scratch_shapes=[pltpu.VMEM(x.shape, jnp.float32) for x in inputs]
        + [
            pltpu.VMEM((PARTS, count, B + R, B), jnp.float32),
            pltpu.SemaphoreType.DMA((4, 2)),
        ],
        compiler_params=pltpu.CompilerParams(vmem_limit_bytes=LIMIT),
        name="local",
    )(*inputs)


def position():
    return lax.axis_index(AXES[0]) * lax.axis_size(AXES[1]) + lax.axis_index(AXES[1])


def is_left(level):
    return (position() >> level) & 1 == 0


def ordered(level, own, other):
    left = is_left(level)
    return jnp.where(left, own, other), jnp.where(left, other, own)


def by_core(here, there):
    low = position() & 1 == 0
    return jnp.where(low, here, there), jnp.where(low, there, here)


def turned(first, second):
    early = left_side(first[: B + R])
    turn = times(early, right_side(second[2 * B + R : 3 * B + R]))
    back = jnp.concatenate(
        [second[B + R : 2 * B + R], turn[:B], turn[B:] + second[3 * B + R :]], axis=0
    )
    return early, back


def joined(first, second):
    early, back = turned(first, second)
    down = times(early, right_side(second[:B]))
    up = mm(back, first[B + R : 2 * B + R])
    return jnp.concatenate(
        [down[:B], down[B:] + second[B : B + R], up[:B], up[B:] + first[2 * B + R :]], axis=0
    )


def store_half(send, pack):
    half = pack.shape[0] // 2
    send[...] = jnp.where(position() & 1 == 0, pack[:half], pack[half:])


def pair_kernel(own, other, pack, send):
    value = joined(*ordered(0, own[...], other[...]))
    pack[...] = value
    store_half(send, value)


def quad_kernel(level, plan, top, *refs):
    own, whole, whole_twin, half, half_twin, one, near, far, pack, send = refs
    partner = dict(zip(plan, by_core(whole[...], whole_twin[...])))
    partner[6 - sum(plan)] = jnp.concatenate(by_core(half[...], half_twin[...]), axis=0)
    one[...] = partner[1]
    mine = joined(*ordered(level, own[...], partner[1]))
    theirs = joined(*ordered(level, partner[2], partner[3]))
    near[...] = mine
    far[...] = theirs
    first, second = ordered(level + 1, mine, theirs)
    if top:
        early, back = turned(first, second)
        down = times(early[B:], right_side(second[:B])) + second[B : B + R]
        up = mm(back[B:], first[B + R : 2 * B + R]) + first[2 * B + R :]
        pack[B : B + R] = down
        left = is_left(level + 2)
        store_half(send, jnp.concatenate([up[:B], jnp.where(left, down, up[B:])], axis=0))
    else:
        value = joined(first, second)
        pack[...] = value
        store_half(send, value)


def combine(kernel, name, own, parts, extra, send_rows):
    whole = jax.ShapeDtypeStruct((PACK, B), jnp.float32)
    return pl.pallas_call(
        kernel,
        out_shape=(whole,) * (1 + extra) + (jax.ShapeDtypeStruct((send_rows, B), jnp.float32),),
        in_specs=[pl.BlockSpec(memory_space=pltpu.VMEM)] * (1 + len(parts)),
        out_specs=[pl.BlockSpec(memory_space=pltpu.VMEM)] * (2 + extra),
        compiler_params=pltpu.CompilerParams(vmem_limit_bytes=LIMIT),
        name=name,
    )(own, *parts)


def advanced(level, first, second, aheads, behinds):
    early, back = turned(first, second)
    late = left_side(back)
    left = is_left(level)
    for part in range(PARTS):
        ahead, behind = aheads[part], behinds[part]
        through = times(late, right_side(behind[:B]))
        through = jnp.concatenate([through[:B], through[B:] + behind[B:]], axis=0)
        onward = times(early, right_side(ahead[:B]))
        onward = jnp.concatenate([onward[:B], onward[B:] + ahead[B:]], axis=0)
        cross = times(early, right_side(behind[B : 2 * B]))
        cross = jnp.concatenate([behind[:B], cross[:B], cross[B:] + behind[2 * B :]], axis=0)
        aheads[part] = jnp.where(left, ahead, onward)
        behinds[part] = jnp.where(left, through, cross)


def prepare_kernel(levels, *refs):
    parts, rows, pairs, (track, spread) = refs[0], refs[1], refs[2:-2], refs[-2:]
    eye = (
        lax.broadcasted_iota(jnp.int32, (B, B), 0) == lax.broadcasted_iota(jnp.int32, (B, B), 1)
    ).astype(jnp.float32)
    none = jnp.zeros((B + R, B), jnp.float32)
    _, back = turned(parts[0], parts[1])
    aheads = [jnp.concatenate([eye, none[:R]], axis=0), parts[0, : B + R]]
    behinds = [back, jnp.concatenate([eye, none], axis=0)]
    for level in range(levels):
        first, second = ordered(level, pairs[2 * level][...], pairs[2 * level + 1][...])
        advanced(level, first, second, aheads, behinds)
    for part in range(PARTS):
        track[part, : B + R] = aheads[part]
        track[part, B + R :] = behinds[part]
        for i in range(rows.shape[1]):
            spread[part, i] = left_side(rows[part, i, : 2 * B])


def prepare(parts, rows, steps):
    return pl.pallas_call(
        lambda *refs: prepare_kernel(len(steps), *refs),
        out_shape=(
            jax.ShapeDtypeStruct((PARTS, PACK, B), jnp.float32),
            jax.ShapeDtypeStruct(rows.shape[:2] + (2 * B, 2 * B), jnp.bfloat16),
        ),
        in_specs=[pl.BlockSpec(memory_space=pltpu.VMEM)] * (2 + 2 * len(steps)),
        out_specs=[pl.BlockSpec(memory_space=pltpu.VMEM)] * 2,
        compiler_params=pltpu.CompilerParams(vmem_limit_bytes=LIMIT),
        cost_estimate=pl.CostEstimate(flops=2**31, bytes_accessed=2**23, transcendentals=0),
        name="prepare",
    )(parts, rows, *(array for step in steps for array in step))


def refine_kernel(start, top, *refs):
    track, pairs, (weights, offsets) = refs[0], refs[1:-2], refs[-2:]
    aheads = [track[part, : B + R] for part in range(PARTS)]
    behinds = [track[part, B + R :] for part in range(PARTS)]
    for i in range(len(pairs) // 2):
        first, second = ordered(start + i, pairs[2 * i][...], pairs[2 * i + 1][...])
        advanced(start + i, first, second, aheads, behinds)
    left = is_left(top)
    for part in range(PARTS):
        ahead, behind = aheads[part], behinds[part]
        weights[part, 0] = right_side(jnp.where(left, behind[:B], behind[B : 2 * B]))
        weights[part, 1] = right_side(jnp.where(left, 0.0, ahead[:B]))
        offsets[part, 0] = behind[2 * B :]
        offsets[part, 1] = ahead[B:]


def refine(start, top, tracked, steps):
    return pl.pallas_call(
        lambda *refs: refine_kernel(start, top, *refs),
        out_shape=(
            jax.ShapeDtypeStruct((PARTS, 2, 2 * B, 2 * B), jnp.bfloat16),
            jax.ShapeDtypeStruct((PARTS, 2, R, B), jnp.float32),
        ),
        in_specs=[pl.BlockSpec(memory_space=pltpu.VMEM)] * (1 + 2 * len(steps)),
        out_specs=[pl.BlockSpec(memory_space=pltpu.VMEM)] * 2,
        compiler_params=pltpu.CompilerParams(vmem_limit_bytes=LIMIT),
        cost_estimate=pl.CostEstimate(flops=2**30, bytes_accessed=2**22, transcendentals=0),
        name="refine",
    )(tracked, *(array for step in steps for array in step))


def finish_kernel(level, own, here, twin, weights, offsets, spread, rows, out_hbm, out, sems):
    got = jnp.concatenate(by_core(here[...], twin[...]), axis=0)
    carry = jnp.where(is_left(level), mm(own[B : B + R], got[:B]), 0.0) + got[B:]
    carry = left_side(carry)
    count = rows.shape[1]
    copies = []
    for part in range(PARTS):
        both = jnp.concatenate(
            [times(carry, weights[part, i]) + offsets[part, i] for i in range(2)], axis=1
        )
        both = jnp.concatenate(halves(both), axis=0)
        for i in range(count):
            wide = jnp.dot(both, spread[part, i], preferred_element_type=jnp.float32)
            wide = wide[:R] + wide[R:]
            out[part * count + i] = rows[part, i, 2 * B :] + wide[:, :B] + wide[:, B:]
            done = part * count + i + 1
            if done % OUT_ROWS == 0:
                span = pl.ds(done - OUT_ROWS, OUT_ROWS)
                copies.append(
                    pltpu.make_async_copy(out.at[span], out_hbm.at[span], sems.at[len(copies)])
                )
                copies[-1].start()
    for copy in copies:
        copy.wait()


def finish(level, own, here, twin, weights, offsets, spread, rows):
    shape = (rows.shape[0] * rows.shape[1], R, B)
    return pl.pallas_call(
        lambda *refs: finish_kernel(level, *refs),
        out_shape=jax.ShapeDtypeStruct(shape, jnp.float32),
        in_specs=[pl.BlockSpec(memory_space=pltpu.VMEM)] * 7,
        out_specs=pl.BlockSpec(memory_space=pltpu.HBM),
        scratch_shapes=[
            pltpu.VMEM(shape, jnp.float32),
            pltpu.SemaphoreType.DMA((shape[0] // OUT_ROWS,)),
        ],
        compiler_params=pltpu.CompilerParams(vmem_limit_bytes=LIMIT),
        name="finish",
    )(own, here, twin, weights, offsets, spread, rows)


def on_device(rhs, pivot_inv, lower_gain, upper_gain):
    devices = lax.axis_size(AXES)
    top = devices.bit_length() - 2
    plane = devices >> 3
    swap = lambda array, even, odd: lax.ppermute(
        array, AXES, [(i, i ^ (odd if i & 1 else even)) for i in range(devices)]
    )
    pack, parts, rows = local(rhs, pivot_inv, lower_gain, upper_gain)
    other = swap(pack, 1, 1)
    steps = [(pack, other)]
    pack, half = combine(pair_kernel, "pair", pack, (other,), 0, PACK // 2)
    for level, plan in PLANS:
        last = level == top - 2
        third = 6 - sum(plan)
        halves = swap(half, third << level, third << level)
        whole = swap(pack, plan[0] << level, plan[1] << level)
        if last:
            aside = prepare(parts, rows, steps)
            whole, aside = lax.optimization_barrier((whole, aside))
        received = (whole, swap(whole, 1, 1), halves, swap(halves, 1, 1))
        own = pack
        one, near, far, pack, half = combine(
            lambda *refs, level=level, plan=plan, last=last: quad_kernel(level, plan, last, *refs),
            f"quad{level}",
            own,
            received,
            3,
            (B + R) // 2 if last else PACK // 2,
        )
        steps += [(own, one), (near, far)]
    facing = [(i, FACING[i // plane] * plane + i % plane) for i in range(devices)]
    got = lax.ppermute(half, AXES, facing)
    tracked, spread = aside
    maps = refine(top - 2, top, tracked, steps[top - 2 :])
    got, maps = lax.optimization_barrier((got, maps))
    return finish(top, pack, got, swap(got, 1, 1), *maps, spread, rows)


def solution(mesh):
    placed = P(AXES, None, None)
    return jax.shard_map(
        on_device,
        mesh=mesh,
        in_specs=(placed,) * 4,
        out_specs=placed,
        check_vma=False,
    )
```

```python
import jax
import jax.numpy as jnp
from jax import lax
from jax.experimental import pallas as pl
from jax.experimental.pallas import tpu as pltpu
from jax.sharding import PartitionSpec as P

AXES = ("wide", "narrow")
B = 128
R = 64
PACK = 3 * B + 2 * R
PARTS = 2
OUT_ROWS = 3
FACING = (6, 7, 4, 5, 2, 3, 0, 1)
PLANS = ((1, (1, 3)), (3, (1, 3)), (5, (1, 3)))
LIMIT = 12 * 2**20


def halves(value):
    high = value.astype(jnp.bfloat16)
    low = (value - high.astype(jnp.float32)).astype(jnp.bfloat16)
    return high, low


def left_side(value):
    return jnp.concatenate(halves(value), axis=1)


def right_side(value):
    both = jnp.concatenate(halves(value), axis=1)
    return jnp.concatenate([both, both], axis=0)


def times(left, right):
    wide = jnp.dot(left, right, preferred_element_type=jnp.float32)
    return wide[:, :B] + wide[:, B:]


def mm(left, right):
    return times(left_side(left), right_side(right))


def local_kernel(
    rhs_hbm,
    pivot_hbm,
    lower_hbm,
    upper_hbm,
    pack,
    parts,
    rows,
    rhs,
    pivot_inv,
    lower,
    upper,
    forward,
    sems,
):
    count = rhs.shape[1]
    pairs = ((pivot_hbm, pivot_inv), (rhs_hbm, rhs), (lower_hbm, lower), (upper_hbm, upper))
    edges = (0, count // 3, count)
    spans = list(zip(edges[:-1], edges[1:]))
    waits = {}

    def fetch(which, slot, start, stop, row):
        source, target = pairs[which]
        span = (slice(None), pl.ds(start, stop - start))
        copy = pltpu.make_async_copy(source.at[span], target.at[span], sems.at[which, slot])
        copy.start()
        waits.setdefault((which // 3, row), []).append(copy)

    for slot, (start, stop) in enumerate(spans):
        for which in range(3):
            fetch(which, slot, start, stop, start)
    fetch(3, 0, 0, count, count - 1)
    states = [None] * PARTS
    scaled = {}
    for i in range(count):
        if (0, i) in waits:
            for copy in waits[0, i]:
                copy.wait()
            stop = next(stop for start, stop in spans if start == i)
            for j in range(i, stop):
                for part in range(PARTS):
                    scaled[part, j] = mm(rhs[part, j], pivot_inv[part, j])
        for part in range(PARTS):
            if i == 0:
                state = jnp.concatenate([-lower[part, 0], scaled[part, 0]], axis=0)
            else:
                moved = mm(states[part], lower[part, i])
                state = jnp.concatenate([-moved[:B], scaled[part, i] - moved[B:]], axis=0)
            forward[part, i] = state
            states[part] = state
    for part in range(PARTS):
        parts[part, : B + R] = states[part]
    for i in range(count - 1, -1, -1):
        for copy in waits.get((1, i), []):
            copy.wait()
        for part in range(PARTS):
            if i == count - 1:
                state = jnp.concatenate([-upper[part, i], states[part]], axis=0)
            else:
                moved = mm(states[part], upper[part, i])
                state = jnp.concatenate([-moved[:B], forward[part, i] - moved[B:]], axis=0)
            rows[part, i] = state
            states[part] = state
    for part in range(PARTS):
        parts[part, B + R :] = states[part]
    pack[...] = joined(parts[0], parts[1])


def local(rhs, pivot_inv, lower, upper):
    inputs = [
        pltpu.with_memory_space_constraint(
            x.reshape((PARTS, x.shape[0] // PARTS) + x.shape[1:]), pltpu.HBM
        )
        for x in (rhs, pivot_inv, lower, upper)
    ]
    count = inputs[0].shape[1]
    return pl.pallas_call(
        local_kernel,
        out_shape=(
            jax.ShapeDtypeStruct((PACK, B), jnp.float32),
            jax.ShapeDtypeStruct((PARTS, PACK, B), jnp.float32),
            jax.ShapeDtypeStruct((PARTS, count, 2 * B + R, B), jnp.float32),
        ),
        in_specs=[pl.BlockSpec(memory_space=pltpu.HBM)] * 4,
        out_specs=[pl.BlockSpec(memory_space=pltpu.VMEM)] * 3,
        scratch_shapes=[pltpu.VMEM(x.shape, jnp.float32) for x in inputs]
        + [
            pltpu.VMEM((PARTS, count, B + R, B), jnp.float32),
            pltpu.SemaphoreType.DMA((4, 2)),
        ],
        compiler_params=pltpu.CompilerParams(vmem_limit_bytes=LIMIT),
        name="local",
    )(*inputs)


def position():
    return lax.axis_index(AXES[0]) * lax.axis_size(AXES[1]) + lax.axis_index(AXES[1])


def is_left(level):
    return (position() >> level) & 1 == 0


def ordered(level, own, other):
    left = is_left(level)
    return jnp.where(left, own, other), jnp.where(left, other, own)


def by_core(here, there):
    low = position() & 1 == 0
    return jnp.where(low, here, there), jnp.where(low, there, here)


def turned(first, second):
    early = left_side(first[: B + R])
    turn = times(early, right_side(second[2 * B + R : 3 * B + R]))
    back = jnp.concatenate(
        [second[B + R : 2 * B + R], turn[:B], turn[B:] + second[3 * B + R :]], axis=0
    )
    return early, back


def joined(first, second):
    early, back = turned(first, second)
    down = times(early, right_side(second[:B]))
    up = mm(back, first[B + R : 2 * B + R])
    return jnp.concatenate(
        [down[:B], down[B:] + second[B : B + R], up[:B], up[B:] + first[2 * B + R :]], axis=0
    )


def store_half(send, pack):
    half = pack.shape[0] // 2
    send[...] = jnp.where(position() & 1 == 0, pack[:half], pack[half:])


def pair_kernel(own, other, pack, send):
    value = joined(*ordered(0, own[...], other[...]))
    pack[...] = value
    store_half(send, value)


def quad_kernel(level, plan, top, *refs):
    own, whole, whole_twin, half, half_twin, one, near, far, pack, send = refs
    partner = dict(zip(plan, by_core(whole[...], whole_twin[...])))
    partner[6 - sum(plan)] = jnp.concatenate(by_core(half[...], half_twin[...]), axis=0)
    one[...] = partner[1]
    mine = joined(*ordered(level, own[...], partner[1]))
    theirs = joined(*ordered(level, partner[2], partner[3]))
    near[...] = mine
    far[...] = theirs
    value = joined(*ordered(level + 1, mine, theirs))
    pack[...] = value
    if top:
        store_half(send, jnp.where(is_left(level + 2), value[: B + R], value[2 * B + R :]))
    else:
        store_half(send, value)


def combine(kernel, name, own, parts, extra, send_rows):
    whole = jax.ShapeDtypeStruct((PACK, B), jnp.float32)
    return pl.pallas_call(
        kernel,
        out_shape=(whole,) * (1 + extra) + (jax.ShapeDtypeStruct((send_rows, B), jnp.float32),),
        in_specs=[pl.BlockSpec(memory_space=pltpu.VMEM)] * (1 + len(parts)),
        out_specs=[pl.BlockSpec(memory_space=pltpu.VMEM)] * (2 + extra),
        compiler_params=pltpu.CompilerParams(vmem_limit_bytes=LIMIT),
        name=name,
    )(own, *parts)


def advanced(level, first, second, aheads, behinds):
    early, back = turned(first, second)
    late = left_side(back)
    left = is_left(level)
    for part in range(PARTS):
        ahead, behind = aheads[part], behinds[part]
        through = times(late, right_side(behind[:B]))
        through = jnp.concatenate([through[:B], through[B:] + behind[B:]], axis=0)
        onward = times(early, right_side(ahead[:B]))
        onward = jnp.concatenate([onward[:B], onward[B:] + ahead[B:]], axis=0)
        cross = times(early, right_side(behind[B : 2 * B]))
        cross = jnp.concatenate([behind[:B], cross[:B], cross[B:] + behind[2 * B :]], axis=0)
        aheads[part] = jnp.where(left, ahead, onward)
        behinds[part] = jnp.where(left, through, cross)


def prepare_kernel(levels, *refs):
    parts, rows, pairs, (track, spread) = refs[0], refs[1], refs[2:-2], refs[-2:]
    eye = (
        lax.broadcasted_iota(jnp.int32, (B, B), 0) == lax.broadcasted_iota(jnp.int32, (B, B), 1)
    ).astype(jnp.float32)
    none = jnp.zeros((B + R, B), jnp.float32)
    _, back = turned(parts[0], parts[1])
    aheads = [jnp.concatenate([eye, none[:R]], axis=0), parts[0, : B + R]]
    behinds = [back, jnp.concatenate([eye, none], axis=0)]
    for level in range(levels):
        first, second = ordered(level, pairs[2 * level][...], pairs[2 * level + 1][...])
        advanced(level, first, second, aheads, behinds)
    for part in range(PARTS):
        track[part, : B + R] = aheads[part]
        track[part, B + R :] = behinds[part]
        for i in range(rows.shape[1]):
            spread[part, i] = left_side(rows[part, i, : 2 * B])


def prepare(parts, rows, steps):
    return pl.pallas_call(
        lambda *refs: prepare_kernel(len(steps), *refs),
        out_shape=(
            jax.ShapeDtypeStruct((PARTS, PACK, B), jnp.float32),
            jax.ShapeDtypeStruct(rows.shape[:2] + (2 * B, 2 * B), jnp.bfloat16),
        ),
        in_specs=[pl.BlockSpec(memory_space=pltpu.VMEM)] * (2 + 2 * len(steps)),
        out_specs=[pl.BlockSpec(memory_space=pltpu.VMEM)] * 2,
        compiler_params=pltpu.CompilerParams(vmem_limit_bytes=LIMIT),
        cost_estimate=pl.CostEstimate(flops=2**31, bytes_accessed=2**23, transcendentals=0),
        name="prepare",
    )(parts, rows, *(array for step in steps for array in step))


def refine_kernel(start, top, *refs):
    track, pairs, (weights, offsets) = refs[0], refs[1:-2], refs[-2:]
    aheads = [track[part, : B + R] for part in range(PARTS)]
    behinds = [track[part, B + R :] for part in range(PARTS)]
    for i in range(len(pairs) // 2):
        first, second = ordered(start + i, pairs[2 * i][...], pairs[2 * i + 1][...])
        advanced(start + i, first, second, aheads, behinds)
    left = is_left(top)
    for part in range(PARTS):
        ahead, behind = aheads[part], behinds[part]
        weights[part, 0] = right_side(jnp.where(left, behind[:B], behind[B : 2 * B]))
        weights[part, 1] = right_side(jnp.where(left, 0.0, ahead[:B]))
        offsets[part, 0] = behind[2 * B :]
        offsets[part, 1] = ahead[B:]


def refine(start, top, tracked, steps):
    return pl.pallas_call(
        lambda *refs: refine_kernel(start, top, *refs),
        out_shape=(
            jax.ShapeDtypeStruct((PARTS, 2, 2 * B, 2 * B), jnp.bfloat16),
            jax.ShapeDtypeStruct((PARTS, 2, R, B), jnp.float32),
        ),
        in_specs=[pl.BlockSpec(memory_space=pltpu.VMEM)] * (1 + 2 * len(steps)),
        out_specs=[pl.BlockSpec(memory_space=pltpu.VMEM)] * 2,
        compiler_params=pltpu.CompilerParams(vmem_limit_bytes=LIMIT),
        cost_estimate=pl.CostEstimate(flops=2**30, bytes_accessed=2**22, transcendentals=0),
        name="refine",
    )(tracked, *(array for step in steps for array in step))


def finish_kernel(level, own, here, twin, weights, offsets, spread, rows, out_hbm, out, sems):
    got = jnp.concatenate(by_core(here[...], twin[...]), axis=0)
    carry = jnp.where(is_left(level), mm(own[B : B + R], got[:B]), 0.0) + got[B:]
    carry = left_side(carry)
    count = rows.shape[1]
    copies = []
    for part in range(PARTS):
        both = jnp.concatenate(
            [times(carry, weights[part, i]) + offsets[part, i] for i in range(2)], axis=1
        )
        both = jnp.concatenate(halves(both), axis=0)
        for i in range(count):
            wide = jnp.dot(both, spread[part, i], preferred_element_type=jnp.float32)
            wide = wide[:R] + wide[R:]
            out[part * count + i] = rows[part, i, 2 * B :] + wide[:, :B] + wide[:, B:]
            done = part * count + i + 1
            if done % OUT_ROWS == 0:
                span = pl.ds(done - OUT_ROWS, OUT_ROWS)
                copies.append(
                    pltpu.make_async_copy(out.at[span], out_hbm.at[span], sems.at[len(copies)])
                )
                copies[-1].start()
    for copy in copies:
        copy.wait()


def finish(level, own, here, twin, weights, offsets, spread, rows):
    shape = (rows.shape[0] * rows.shape[1], R, B)
    return pl.pallas_call(
        lambda *refs: finish_kernel(level, *refs),
        out_shape=jax.ShapeDtypeStruct(shape, jnp.float32),
        in_specs=[pl.BlockSpec(memory_space=pltpu.VMEM)] * 7,
        out_specs=pl.BlockSpec(memory_space=pltpu.HBM),
        scratch_shapes=[
            pltpu.VMEM(shape, jnp.float32),
            pltpu.SemaphoreType.DMA((shape[0] // OUT_ROWS,)),
        ],
        compiler_params=pltpu.CompilerParams(vmem_limit_bytes=LIMIT),
        name="finish",
    )(own, here, twin, weights, offsets, spread, rows)


def on_device(rhs, pivot_inv, lower_gain, upper_gain):
    devices = lax.axis_size(AXES)
    top = devices.bit_length() - 2
    plane = devices >> 3
    swap = lambda array, even, odd: lax.ppermute(
        array, AXES, [(i, i ^ (odd if i & 1 else even)) for i in range(devices)]
    )
    pack, parts, rows = local(rhs, pivot_inv, lower_gain, upper_gain)
    other = swap(pack, 1, 1)
    steps = [(pack, other)]
    pack, half = combine(pair_kernel, "pair", pack, (other,), 0, PACK // 2)
    for level, plan in PLANS:
        last = level == top - 2
        third = 6 - sum(plan)
        halves = swap(half, third << level, third << level)
        whole = swap(pack, plan[0] << level, plan[1] << level)
        if last:
            aside = prepare(parts, rows, steps)
            whole, aside = lax.optimization_barrier((whole, aside))
        received = (whole, swap(whole, 1, 1), halves, swap(halves, 1, 1))
        own = pack
        one, near, far, pack, half = combine(
            lambda *refs, level=level, plan=plan, last=last: quad_kernel(level, plan, last, *refs),
            f"quad{level}",
            own,
            received,
            3,
            (B + R) // 2 if last else PACK // 2,
        )
        steps += [(own, one), (near, far)]
    facing = [(i, FACING[i // plane] * plane + i % plane) for i in range(devices)]
    got = lax.ppermute(half, AXES, facing)
    tracked, spread = aside
    maps = refine(top - 2, top, tracked, steps[top - 2 :])
    got, maps = lax.optimization_barrier((got, maps))
    return finish(top, pack, got, swap(got, 1, 1), *maps, spread, rows)


def solution(mesh):
    placed = P(AXES, None, None)
    return jax.shard_map(
        on_device,
        mesh=mesh,
        in_specs=(placed,) * 4,
        out_specs=placed,
        check_vma=False,
    )
```
